512 devices in a mesh: row: 16 (over x, y_lo, core), col: 32 (over y_hi, z).
Axes of the slice: x: 4, y: 8 (y_hi: 4, y_lo: 2; y = y_hi * 2 + y_lo), z: 8, core: 2. Of those that a mesh axis runs over, the one named last changes fastest.
Arguments:
- specimen: float32 [2, 4096, 8192], P(None, 'row', 'col'), may hold values from -6 to 6
- probe_field: float32 [2, 256, 256], replicated, may hold values from -5 to 5
- offsets: int32 [16, 32, 3, 2], P('row', 'col'), may hold values from -128 to 128
- amplitudes: float32 [16, 32, 3, 256, 256], P('row', 'col'), may hold values from 0.5 to 2.5
Outputs:
- updated: float32 [2, 4096, 8192], P(None, 'row', 'col')
The draws below stay inside these ranges and needn't reach their ends.
Inputs may be any that keep to these rules, and one draw needn't show every extreme that they name: Window p of tile (r, c) starts at row r * 256 + offsets[r, c, p, 0] and column c * 256 + offsets[r, c, p, 1]; windows may reach past the specimen's border, where the object is zero.
All inputs are finite; a program needn't handle non-finite values.
Results may differ from the reference program's by a relative error of at most 0.0003.
Values sent between devices are 32-bit elements; how exact they have to be, the bound alone decides.
A program may use at most 64 MiB of HBM per device.

```python
import math
import jax
import jax.numpy as jnp
from jax import lax

TILE = 256
WIN = 256
HALO = 128
POS = 3
ITERS = 2
ROW_TILES = 16
COL_TILES = 32
OBJ_ROWS = 4096
OBJ_COLS = 8192


def place_ends(drawn, rng, low, largest):
    longest = drawn.shape.index(max(drawn.shape))
    spots = []
    for shift in (0, 1):
        where = [jax.random.randint(jax.random.fold_in(rng, axis), (), 0, length) for axis, length in enumerate(drawn.shape)]
        where[longest] = (where[longest] + shift) % drawn.shape[longest]
        spots.append(tuple(where))
    return drawn.at[spots[0]].set(low).at[spots[1]].set(largest)


def block_scale(rng, extent, pieces, low, top_value):
    loudness = 1.0
    for dim, parts in pieces:
        draws = jax.random.uniform(jax.random.fold_in(jax.random.fold_in(rng, 6), dim), (parts,), jnp.float32, low / len(pieces), top_value / len(pieces))
        loudness = loudness * jnp.repeat(jnp.exp(draws), extent[dim] // parts).reshape((-1,) + (1,) * (len(extent) - 1 - dim))
    return loudness


def centred(rng, extent, deviation, most, pieces=(), kind=jnp.bfloat16):
    values = jax.random.normal(rng, extent, jnp.float32) * deviation
    if len(pieces) > 0:
        values = block_scale(rng, extent, pieces, -0.22, 0.18) * values
    return jnp.clip(values, min=-most, max=most).astype(kind)


def setup_inputs(seed: int = 0) -> dict:
    key_of = jax.random.split(jax.random.key(seed), 5)
    return {
        "specimen": centred(key_of[0], (2, OBJ_ROWS, OBJ_COLS), 1.0, 6.0, ((1, 16), (2, 32)), jnp.float32),
        "probe_field": centred(key_of[1], (2, WIN, WIN), 0.7, 5.0, (), jnp.float32),
        "offsets": place_ends(jax.random.randint(key_of[2], (ROW_TILES, COL_TILES, POS, 2), 0 - HALO, TILE + HALO - WIN + 1), jax.random.fold_in(key_of[2], 1), 0 - HALO, TILE + HALO - WIN).astype(jnp.int32),
        "amplitudes": jnp.clip(0.5 + 2.0 * jax.random.uniform(key_of[3], (ROW_TILES, COL_TILES, POS, WIN, WIN), jnp.float32) ** block_scale(key_of[3], (ROW_TILES, COL_TILES, POS, WIN, WIN), ((0, 16), (1, 32)), -0.2, 0.2), 0.5, 2.5),
    }


smooth_term = 0.25
ridge_share = 0.1

def dft_tables(length):
    counter = jnp.arange(length, dtype=jnp.int32)
    product = counter[:, None] * counter[None, :] % length
    angle = product.astype(jnp.float32) * (2.0 * math.pi / length)
    scale = 1.0 / math.sqrt(length)
    return (jnp.cos(angle) * scale, -jnp.sin(angle) * scale)

def mat_left(matrix, stacked):
    return jnp.einsum('kn,pnm->pkm', matrix, stacked, precision=lax.Precision.HIGHEST)

def mat_right(stacked, matrix):
    return jnp.einsum('pnm,mk->pnk', stacked, matrix, precision=lax.Precision.HIGHEST)

def transform(cos_table, sin_table, real_part, imag_part):
    real_mid = mat_left(cos_table, real_part) - mat_left(sin_table, imag_part)
    imag_mid = mat_left(cos_table, imag_part) + mat_left(sin_table, real_part)
    real_out = mat_right(real_mid, cos_table) - mat_right(imag_mid, sin_table)
    imag_out = mat_right(imag_mid, cos_table) + mat_right(real_mid, sin_table)
    return (real_out, imag_out)

def window_gradient(probe_field, patch_real, patch_imag, amplitude, cos_table, sin_table):
    probe_real = probe_field[0]
    probe_imag = probe_field[1]
    exit_real = probe_real * patch_real - probe_imag * patch_imag
    exit_imag = probe_real * patch_imag + probe_imag * patch_real
    far_real, far_imag = transform(cos_table, sin_table, exit_real, exit_imag)
    modulus = jnp.sqrt(far_real * far_real + far_imag * far_imag + smooth_term)
    factor = 1.0 - amplitude / modulus
    back_real, back_imag = transform(cos_table, -sin_table, factor * far_real, factor * far_imag)
    grad_real = probe_real * back_real + probe_imag * back_imag
    grad_imag = probe_real * back_imag - probe_imag * back_real
    return (grad_real, grad_imag)

def reference(specimen, probe_field, offsets, amplitudes):
    cos_table, sin_table = dft_tables(WIN)
    device_count = ROW_TILES * COL_TILES
    flat_offsets = offsets.reshape(device_count, POS, 2)
    flat_amplitudes = amplitudes.reshape(device_count, POS, WIN, WIN)
    intensity = probe_field[0] * probe_field[0] + probe_field[1] * probe_field[1]
    zero_index = jnp.zeros((), jnp.int32)
    devices = jnp.arange(device_count, dtype=jnp.int32)

    def corner(device, position):
        row_block = device // COL_TILES
        col_block = device % COL_TILES
        top = (row_block * TILE + HALO + flat_offsets[device, position, 0]).astype(jnp.int32)
        left = (col_block * TILE + HALO + flat_offsets[device, position, 1]).astype(jnp.int32)
        return (top, left)

    def add_light(light, device):
        for position in range(POS):
            top, left = corner(device, position)
            block = lax.dynamic_slice(light, (top, left), (WIN, WIN))
            light = lax.dynamic_update_slice(light, block + intensity, (top, left))
        return (light, None)
    light_full = jnp.zeros((OBJ_ROWS + 2 * HALO, OBJ_COLS + 2 * HALO), jnp.float32)
    light_full, unused = lax.scan(add_light, light_full, devices)
    light_inner = light_full[HALO:HALO + OBJ_ROWS, HALO:HALO + OBJ_COLS]
    light_peak = jnp.max(light_inner)
    divisor = light_inner + ridge_share * light_peak
    padded = jnp.pad(specimen, ((0, 0), (HALO, HALO), (HALO, HALO)))
    for iteration in range(ITERS):

        def add_gradient(gradient, device):
            corners = [corner(device, position) for position in range(POS)]
            patches = jnp.stack([lax.dynamic_slice(padded, (zero_index, top, left), (2, WIN, WIN)) for top, left in corners])
            grad_real, grad_imag = window_gradient(probe_field, patches[:, 0], patches[:, 1], flat_amplitudes[device], cos_table, sin_table)
            for position in range(POS):
                top, left = corners[position]
                block = lax.dynamic_slice(gradient, (zero_index, top, left), (2, WIN, WIN))
                piece = jnp.stack([grad_real[position], grad_imag[position]])
                gradient = lax.dynamic_update_slice(gradient, block + piece, (zero_index, top, left))
            return (gradient, None)
        gradient = jnp.zeros(padded.shape, jnp.float32)
        gradient, unused = lax.scan(add_gradient, gradient, devices)
        inner = padded[:, HALO:HALO + OBJ_ROWS, HALO:HALO + OBJ_COLS] - gradient[:, HALO:HALO + OBJ_ROWS, HALO:HALO + OBJ_COLS] / divisor[None]
        padded = jnp.pad(inner, ((0, 0), (HALO, HALO), (HALO, HALO)))
    return padded[:, HALO:HALO + OBJ_ROWS, HALO:HALO + OBJ_COLS]
```

```python
import functools
import math

import jax
import jax.numpy as jnp
import ml_dtypes
import numpy as np
from jax import lax
from jax.experimental import pallas as pl
from jax.experimental.pallas import tpu as pltpu
from jax.sharding import PartitionSpec as P

WIN = 256
HALF = 128
HALO = 128
ITERS = 2
SMOOTH = 0.25
RIDGE = 0.1
MESH = pl.DeviceIdType.MESH

NEIGHBOURS = [(a, b) for a in (-1, 0, 1) for b in (-1, 0, 1) if (a, b) != (0, 0)]


def dft_tables():
    n = np.arange(HALF)[None, :]
    m = np.arange(HALF)[:, None]
    blocks = []
    for freq in (2 * m, 2 * m + 1):
        angle = -2.0 * math.pi * ((freq * n) % WIN) / WIN
        re, im = np.cos(angle) / 16.0, np.sin(angle) / 16.0
        blocks.append(np.block([[re, -im], [im, re]]))
    out = []
    for block in (blocks[0], blocks[1], blocks[0].T, blocks[1].T):
        high = block.astype(ml_dtypes.bfloat16)
        low = (block - high.astype(np.float64)).astype(ml_dtypes.bfloat16)
        out += [high, low]
    order = np.concatenate([np.arange(0, WIN, 2), np.arange(1, WIN, 2)])
    perm = (order[:, None] == np.arange(WIN)[None, :]).astype(ml_dtypes.bfloat16)
    out += [perm, perm.T]
    return np.stack(out)


def split(x):
    high = x.astype(jnp.bfloat16)
    low = (x - high.astype(jnp.float32)).astype(jnp.bfloat16)
    return high, low


def dot(a, b):
    return jnp.dot(a, b, preferred_element_type=jnp.float32)


def left(tab, index, x):
    high, low = split(x)
    th, tl = tab[2 * index], tab[2 * index + 1]
    return dot(jnp.concatenate([th, th, tl], axis=1), jnp.concatenate([high, low, high], axis=0))


def right(x, tab, index):
    high, low = split(x)
    th, tl = tab[2 * index], tab[2 * index + 1]
    return dot(jnp.concatenate([high, low, high], axis=1), jnp.concatenate([th, th, tl], axis=0))


def digits(size, part):
    return (size // part, part) if size > part else (1, size)


def kernel(
    n_row, n_col, n_pos,
    spec, probe_in, off, amp_in, tab_in,
    out,
    span_a, span_b, grad, wide, pad, light, inv, probe, amp, tab, noff, row_in, col_in, peak_out, peak_in,
    local_sem, off_sem, span_send, span_recv, fold_send, fold_recv, peak_send, peak_recv,
):
    r, c = lax.axis_index("row"), lax.axis_index("col")
    f32 = jnp.float32
    spans = (span_a, span_b)
    lane = lax.broadcasted_iota(jnp.int32, (1, HALF), 1)

    def exists(dr, dc):
        ok = None
        for index, step, size in ((r, dr, n_row), (c, dc, n_col)):
            if step:
                here = (index + step >= 0) & (index + step < size)
                ok = here if ok is None else ok & here
        return ok

    ra, rb = digits(n_row, 4)
    ca, cb = digits(n_col, 8)
    groups = []
    for phase, (size, place) in enumerate(
        (
            (rb, lambda j: {"row": (r // rb) * rb + (r % rb + j) % rb, "col": c}),
            (cb, lambda j: {"row": r, "col": (c // cb) * cb + (c % cb + j) % cb}),
            (ra, lambda j: {"row": ((r // rb + j) % ra) * rb + r % rb, "col": c}),
            (ca, lambda j: {"row": r, "col": ((c // cb + j) % ca) * cb + c % cb}),
        )
    ):
        groups.append([(j, place(j)) for j in range(1, size)])

    for k in range(9):
        for p in range(n_pos):
            for d in range(2):
                if k == 4:
                    noff[k, p, d] = off[0, 0, p, d]
                else:
                    noff[k, p, d] = 4096

    for k in range(2):
        for dr, dc, place in (
            (-1, 0, (slice(None), pl.ds(0, HALO))),
            (1, 0, (slice(None), pl.ds(HALO + WIN, HALO))),
            (0, -1, (0, pl.ds(HALO, WIN))),
            (0, 1, (3, pl.ds(HALO, WIN))),
        ):
            @pl.when(jnp.logical_not(exists(dr, dc)))
            def _(k=k, place=place):
                ref = spans[k].at[(slice(None),) + place + (slice(None),)]
                ref[...] = jnp.zeros(ref.shape, f32)

    barrier = pltpu.get_barrier_semaphore()
    total = 0
    for dr, dc in NEIGHBOURS:
        here = exists(dr, dc)
        total = total + here.astype(jnp.int32)

        @pl.when(here)
        def _(dr=dr, dc=dc):
            pl.semaphore_signal(barrier, inc=1, device_id={"row": r + dr, "col": c + dc}, device_id_type=MESH)

    for group in groups:
        for j, place in group:
            pl.semaphore_signal(barrier, inc=1, device_id=place, device_id_type=MESH)
            total = total + 1

    copies = [
        pltpu.make_async_copy(spec.at[:, :, pl.ds(0, HALF)], span_a.at[:, 1, pl.ds(HALO, WIN), :], local_sem.at[0]),
        pltpu.make_async_copy(spec.at[:, :, pl.ds(HALF, HALF)], span_a.at[:, 2, pl.ds(HALO, WIN), :], local_sem.at[1]),
        pltpu.make_async_copy(probe_in, probe, local_sem.at[2]),
        pltpu.make_async_copy(tab_in, tab, local_sem.at[3]),
        pltpu.make_async_copy(amp_in.at[0, 0], amp, local_sem.at[4]),
    ]
    for copy in copies:
        copy.start()

    pl.semaphore_wait(barrier, total)

    def remote(src, dst, send, recv, dr, dc):
        return pltpu.make_async_remote_copy(
            src, dst, send, recv, device_id={"row": r + dr, "col": c + dc}, device_id_type=MESH
        )

    def start(copy, dr, dc):
        @pl.when(exists(dr, dc))
        def _():
            copy.start()

    def finish(copy, dr, dc):
        @pl.when(exists(dr, dc))
        def _():
            copy.wait_send()

        @pl.when(exists(-dr, -dc))
        def _():
            copy.wait_recv()

    def widen_col(k):
        out_copies = []
        for i, (dc, tile, there) in enumerate(((-1, 1, 3), (1, 2, 0))):
            if k == 0:
                src = spec.at[:, :, pl.ds((tile - 1) * HALF, HALF)]
            else:
                src = spans[k].at[:, tile, pl.ds(HALO, WIN), :]
            dst = spans[k].at[:, there, pl.ds(HALO, WIN), :]
            copy = remote(src, dst, span_send.at[k, i], span_recv.at[k, i], 0, dc)
            start(copy, 0, dc)
            out_copies.append((copy, 0, dc))
        return out_copies

    def widen_row(k):
        out_copies = []
        for i, (dr, here, there) in enumerate(((-1, HALO, HALO + WIN), (1, WIN, 0))):
            src = spans[k].at[:, :, pl.ds(here, HALO), :]
            dst = spans[k].at[:, :, pl.ds(there, HALO), :]
            copy = remote(src, dst, span_send.at[k, 2 + i], span_recv.at[k, 2 + i], dr, 0)
            start(copy, dr, 0)
            out_copies.append((copy, dr, 0))
        return out_copies

    first = widen_col(0)
    off_copies = []
    for i, (dr, dc) in enumerate(NEIGHBOURS):
        slot = (-dr + 1) * 3 + (-dc + 1)
        copy = remote(off.at[0, 0], noff.at[slot], off_sem.at[0, i], off_sem.at[1, i], dr, dc)
        start(copy, dr, dc)
        off_copies.append((copy, dr, dc))

    def clear(ref, count):
        def body(i, _):
            ref[i] = jnp.zeros(ref.shape[1:], f32)
            return 0

        lax.fori_loop(0, count, body, 0)

    clear(pad, 7)
    copies[2].wait()
    copies[0].wait()
    copies[1].wait()
    for t in range(2):
        cols = pl.ds(t * HALF, HALF)
        pad[2 + t, pl.ds(WIN, WIN), :] = probe[0, :, cols] * probe[0, :, cols] + probe[1, :, cols] * probe[1, :, cols]

    def clear_wide(i, _):
        p, rest = i // 12, i % 12
        wide[p, rest // 6, rest % 6] = jnp.zeros((3 * WIN, HALF), f32)
        return 0

    lax.fori_loop(0, n_pos * 12, clear_wide, 0)

    for item in first:
        finish(*item)
    second = widen_row(0)

    for item in off_copies:
        finish(*item)

    light[...] = jnp.zeros(light.shape, f32)

    def add_light(i, _):
        near, p = i // n_pos, i % n_pos
        top = jnp.clip(noff[near, p, 0] + (near // 3 - 1) * WIN, -WIN, WIN)
        side = jnp.clip(noff[near, p, 1] + (near % 3 - 1) * WIN, -WIN, WIN)
        rows = pl.ds(WIN - top, WIN)
        start_col = WIN - side
        q, s = start_col // HALF, start_col % HALF
        turn = (HALF - s) % HALF
        rolled = [pltpu.roll(pad[q + j, rows, :], turn, 1) for j in range(3)]
        keep = lane < HALF - s
        for t in range(2):
            light[t] = light[t] + jnp.where(keep, rolled[t], rolled[t + 1])
        return 0

    lax.fori_loop(0, 9 * n_pos, add_light, 0)

    peak = jnp.max(light[...].reshape(2 * WIN // 8, 8, HALF), axis=0)

    def peak_start(phase, value):
        peak_out[phase] = value
        items = []
        for j, place in groups[phase]:
            copy = pltpu.make_async_remote_copy(
                peak_out.at[phase], peak_in.at[phase, j], peak_send.at[phase, j], peak_recv.at[phase, j],
                device_id=place, device_id_type=MESH,
            )
            copy.start()
            items.append(copy)
        return items

    def peak_finish(phase, items):
        for copy in items:
            copy.wait()
        value = peak_out[phase]
        for j, _ in groups[phase]:
            value = jnp.maximum(value, peak_in[phase, j])
        return value

    items = peak_start(0, peak)

    copies[3].wait()
    copies[4].wait()

    def order_amp(p, _):
        rows = tab[8]
        high, low = split(amp[p])
        x = dot(jnp.concatenate([rows, rows], axis=1), jnp.concatenate([high, low], axis=0))
        high, low = split(x)
        cols = tab[9]
        amp[p] = dot(jnp.concatenate([high, low], axis=1), jnp.concatenate([cols, cols], axis=0))
        return 0

    lax.fori_loop(0, n_pos, order_amp, 0)
    peak = peak_finish(0, items)
    items = peak_start(1, peak)

    for item in second:
        finish(*item)

    def cat(a, b, axis):
        return jnp.concatenate([a, b], axis=axis)

    def window(k, p):
        top = off[0, 0, p, 0] + HALO
        side = off[0, 0, p, 1] + HALO
        q, s = side // HALF, side % HALF
        rows = pl.ds(top, WIN)
        turn = (HALF - s) % HALF
        keep = lane < HALF - s
        patch = []
        for part in range(2):
            rolled = [
                pltpu.roll(spans[k][part, jnp.minimum(q + j, 3), rows, :], turn, 1) for j in range(3)
            ]
            patch.append(cat(jnp.where(keep, rolled[0], rolled[1]), jnp.where(keep, rolled[1], rolled[2]), 1))
        pr, pi = probe[0], probe[1]
        er = pr * patch[0] - pi * patch[1]
        ei = pr * patch[1] + pi * patch[0]
        sums = cat(er[:HALF] + er[HALF:], ei[:HALF] + ei[HALF:], 0)
        difs = cat(er[:HALF] - er[HALF:], ei[:HALF] - ei[HALF:], 0)
        even = left(tab, 0, sums)
        odd = left(tab, 1, difs)
        xr = cat(even[:HALF], odd[:HALF], 0)
        xi = cat(even[HALF:], odd[HALF:], 0)
        sums = cat(xr[:, :HALF] + xr[:, HALF:], xi[:, :HALF] + xi[:, HALF:], 1)
        difs = cat(xr[:, :HALF] - xr[:, HALF:], xi[:, :HALF] - xi[:, HALF:], 1)
        out_cols = []
        for index, x in ((0, sums), (1, difs)):
            far = right(x, tab, 2 + index)
            fr, fi = far[:, :HALF], far[:, HALF:]
            factor = 1.0 - amp[p, :, pl.ds(index * HALF, HALF)] * lax.rsqrt(fr * fr + fi * fi + SMOOTH)
            out_cols.append(right(cat(factor * fr, factor * fi, 1), tab, index))
        lo, hi = out_cols[0] + out_cols[1], out_cols[0] - out_cols[1]
        xr = cat(lo[:, :HALF], hi[:, :HALF], 1)
        xi = cat(lo[:, HALF:], hi[:, HALF:], 1)
        even = left(tab, 2, cat(xr[:HALF], xi[:HALF], 0))
        odd = left(tab, 3, cat(xr[HALF:], xi[HALF:], 0))
        lo, hi = even + odd, even - odd
        br = cat(lo[:HALF], hi[:HALF], 0)
        bi = cat(lo[HALF:], hi[HALF:], 0)
        g = (pr * br + pi * bi, pr * bi - pi * br)
        past = lane >= s
        zero = jnp.zeros((WIN, HALF), f32)
        for part in range(2):
            one = pltpu.roll(g[part][:, :HALF], s, 1)
            two = pltpu.roll(g[part][:, HALF:], s, 1)
            wide[p, part, 2, pl.ds(WIN, WIN), :] = jnp.where(past, one, zero)
            wide[p, part, 3, pl.ds(WIN, WIN), :] = jnp.where(past, two, one)
            wide[p, part, 4, pl.ds(WIN, WIN), :] = jnp.where(past, zero, two)

    def gather(k):
        def body(i, _):
            part, t = i // 4, i % 4
            for chunk in range(4):
                acc = None
                for p in range(n_pos):
                    top = off[0, 0, p, 0] + HALO
                    q = (off[0, 0, p, 1] + HALO) // HALF
                    piece = wide[p, part, 2 + t - q, pl.ds(WIN - top + chunk * HALF, HALF), :]
                    acc = piece if acc is None else acc + piece
                grad[k, part, t, pl.ds(chunk * HALF, HALF), :] = acc
            return 0

        lax.fori_loop(0, 8, body, 0)

    for k in range(ITERS):
        lax.fori_loop(0, n_pos, lambda p, _, k=k: (window(k, p), 0)[1], 0)
        gather(k)

        sent = []
        for i, (dr, here) in enumerate(((-1, 0), (1, HALO + WIN))):
            copy = remote(
                grad.at[k, :, :, pl.ds(here, HALO), :], row_in.at[k, i], fold_send.at[k, i], fold_recv.at[k, i], dr, 0
            )
            start(copy, dr, 0)
            sent.append((copy, dr, 0))
        if k == 0:
            peak = peak_finish(1, items)
            items = peak_start(2, peak)
        for i, (copy, dr, dc) in enumerate(sent):
            finish(copy, dr, dc)
            rows = pl.ds(WIN, HALO) if dr < 0 else pl.ds(HALO, HALO)

            @pl.when(exists(-dr, 0))
            def _(i=i, rows=rows):
                for part in range(2):
                    for t in range(4):
                        grad[k, part, t, rows, :] = grad[k, part, t, rows, :] + row_in[k, i, part, t]

        sent = []
        for i, (dc, here) in enumerate(((-1, 0), (1, 3))):
            copy = remote(
                grad.at[k, :, here, pl.ds(HALO, WIN), :], col_in.at[k, i],
                fold_send.at[k, 2 + i], fold_recv.at[k, 2 + i], 0, dc,
            )
            start(copy, 0, dc)
            sent.append((copy, 0, dc))
        if k == 0:
            peak = peak_finish(2, items)
            items = peak_start(3, peak)
            peak = jnp.max(peak_finish(3, items))
            inv[...] = 1.0 / (light[...] + RIDGE * peak)
        for i, (copy, dr, dc) in enumerate(sent):
            finish(copy, dr, dc)
            t = 2 if dc < 0 else 1

            @pl.when(exists(0, -dc))
            def _(i=i, t=t):
                for part in range(2):
                    grad[k, part, t, pl.ds(HALO, WIN), :] = grad[k, part, t, pl.ds(HALO, WIN), :] + col_in[k, i, part]

        for t in range(2):
            for part in range(2):
                new = spans[k][part, 1 + t, pl.ds(HALO, WIN), :] - grad[k, part, 1 + t, pl.ds(HALO, WIN), :] * inv[t]
                if k + 1 < ITERS:
                    spans[k + 1][part, 1 + t, pl.ds(HALO, WIN), :] = new
                else:
                    out[part, :, pl.ds(t * HALF, HALF)] = new
        if k + 1 < ITERS:
            for item in widen_col(k + 1):
                finish(*item)
            for item in widen_row(k + 1):
                finish(*item)


def solution(mesh):
    n_row, n_col = mesh.shape["row"], mesh.shape["col"]
    tables = dft_tables()

    def local(specimen, probe_field, offsets, amplitudes):
        n_pos = offsets.shape[2]
        vmem = lambda *shape: pltpu.VMEM(shape, jnp.float32)
        dma = lambda *shape: pltpu.SemaphoreType.DMA(shape)
        return pl.pallas_call(
            functools.partial(kernel, n_row, n_col, n_pos),
            out_shape=jax.ShapeDtypeStruct((2, WIN, WIN), jnp.float32),
            in_specs=[
                pl.BlockSpec(memory_space=pl.ANY),
                pl.BlockSpec(memory_space=pl.ANY),
                pl.BlockSpec(memory_space=pltpu.SMEM),
                pl.BlockSpec(memory_space=pl.ANY),
                pl.BlockSpec(memory_space=pl.ANY),
            ],
            out_specs=pl.BlockSpec(memory_space=pltpu.VMEM),
            scratch_shapes=[
                vmem(2, 4, 512, HALF),
                vmem(2, 4, 512, HALF),
                vmem(ITERS, 2, 4, 512, HALF),
                vmem(n_pos, 2, 6, 3 * WIN, HALF),
                vmem(7, 3 * WIN, HALF),
                vmem(2, WIN, HALF),
                vmem(2, WIN, HALF),
                vmem(2, WIN, WIN),
                vmem(n_pos, WIN, WIN),
                pltpu.VMEM((10, WIN, WIN), jnp.bfloat16),
                pltpu.SMEM((9, n_pos, 2), jnp.int32),
                vmem(ITERS, 2, 2, 4, HALO, HALF),
                vmem(ITERS, 2, 2, WIN, HALF),
                vmem(4, 8, HALF),
                vmem(4, 8, 8, HALF),
                dma(5),
                dma(2, 8),
                dma(ITERS, 4),
                dma(ITERS, 4),
                dma(ITERS, 4),
                dma(ITERS, 4),
                dma(4, 8),
                dma(4, 8),
            ],
            compiler_params=pltpu.CompilerParams(
                collective_id=0, has_side_effects=True, vmem_limit_bytes=56 * 1024 * 1024
            ),
        )(specimen, probe_field, offsets, amplitudes, jnp.asarray(tables))

    return jax.shard_map(
        local,
        mesh=mesh,
        in_specs=(
            P(None, "row", "col"),
            P(),
            P("row", "col", None, None),
            P("row", "col", None, None, None),
        ),
        out_specs=P(None, "row", "col"),
        check_vma=False,
    )
```

```python
import functools
import math

import jax
import jax.numpy as jnp
import ml_dtypes
import numpy as np
from jax import lax
from jax.experimental import pallas as pl
from jax.experimental.pallas import tpu as pltpu
from jax.sharding import PartitionSpec as P

WIN = 256
HALF = 128
HALO = 128
ITERS = 2
SMOOTH = 0.25
RIDGE = 0.1
MESH = pl.DeviceIdType.MESH

NEIGHBOURS = [(a, b) for a in (-1, 0, 1) for b in (-1, 0, 1) if (a, b) != (0, 0)]


def dft_tables():
    n = np.arange(HALF)[None, :]
    m = np.arange(HALF)[:, None]
    blocks = []
    for freq in (2 * m, 2 * m + 1):
        angle = -2.0 * math.pi * ((freq * n) % WIN) / WIN
        re, im = np.cos(angle) / 16.0, np.sin(angle) / 16.0
        blocks.append(np.block([[re, -im], [im, re]]))
    out = []
    for block in (blocks[0], blocks[1], blocks[0].T, blocks[1].T):
        high = block.astype(ml_dtypes.bfloat16)
        low = (block - high.astype(np.float64)).astype(ml_dtypes.bfloat16)
        out += [high, low]
    order = np.concatenate([np.arange(0, WIN, 2), np.arange(1, WIN, 2)])
    perm = (order[:, None] == np.arange(WIN)[None, :]).astype(ml_dtypes.bfloat16)
    out += [perm, perm.T]
    return np.stack(out)


def split(x):
    high = x.astype(jnp.bfloat16)
    low = (x - high.astype(jnp.float32)).astype(jnp.bfloat16)
    return high, low


def dot(a, b):
    return jnp.dot(a, b, preferred_element_type=jnp.float32)


def left(tab, index, x):
    high, low = split(x)
    th, tl = tab[2 * index], tab[2 * index + 1]
    return dot(jnp.concatenate([th, th, tl], axis=1), jnp.concatenate([high, low, high], axis=0))


def right(x, tab, index):
    high, low = split(x)
    th, tl = tab[2 * index], tab[2 * index + 1]
    return dot(jnp.concatenate([high, low, high], axis=1), jnp.concatenate([th, th, tl], axis=0))


def digits(size, part):
    return (size // part, part) if size > part else (1, size)


Z_LEN = 8
CHUNKS = 2


class Message:
    def __init__(self, pool, device, send_if, recv_if, src, dst):
        send, recv, index = pool[0], pool[1], pool[2]
        pool[2] += 1
        self.send_if, self.recv_if = send_if, recv_if
        self.copy = pltpu.make_async_remote_copy(
            src, dst, send.at[index], recv.at[index], device_id=device, device_id_type=MESH
        )

    def _when(self, cond, action):
        if cond is None:
            action()
        else:
            pl.when(cond)(action)

    def start(self):
        self._when(self.send_if, self.copy.start)

    def recv(self):
        self._when(self.recv_if, self.copy.wait_recv)

    def sent(self):
        self._when(self.send_if, self.copy.wait_send)


def kernel(
    n_row, n_col, n_pos,
    spec, probe_in, off, amp_in, tab_in,
    out,
    span_a, span_b, grad, wide, pad, light, inv, probe, amp, tab, noff,
    corner_in, core_in, row_in, col_in, relay_strip, relay_corner, peak_out, peak_in,
    local_sem, off_sem, send_sem, recv_sem, peak_send, peak_recv,
):
    r, c = lax.axis_index("row"), lax.axis_index("col")
    f32 = jnp.float32
    spans = (span_a, span_b)
    lane = lax.broadcasted_iota(jnp.int32, (1, HALF), 1)
    pool = [send_sem, recv_sem, 0]

    odd = r % 2
    near = pl.multiple_of(HALO + HALF - HALF * odd, HALF)
    far = pl.multiple_of(HALO + HALF * odd, HALF)
    inner = pl.multiple_of((HALO + WIN) * (1 - odd), HALF)
    outer = pl.multiple_of((HALO + WIN) * odd, HALF)
    partner = {"row": r + 1 - 2 * odd, "col": c}
    r_out = r - 1 + 2 * odd
    has_outer = (r_out >= 0) & (r_out < n_row)
    beyond = {"row": r_out, "col": c}

    def exists(dr, dc):
        ok = None
        for index, step, size in ((r, dr, n_row), (c, dc, n_col)):
            if step:
                here = (index + step >= 0) & (index + step < size)
                ok = here if ok is None else ok & here
        return ok

    def col_ok(x):
        return (x >= 0) & (x < n_col)

    ra, rb = digits(n_row, 4)
    ca, cb = digits(n_col, Z_LEN)
    groups = []
    for size, place in (
        (rb, lambda j: {"row": (r // rb) * rb + (r % rb + j) % rb, "col": c}),
        (cb, lambda j: {"row": r, "col": (c // cb) * cb + (c % cb + j) % cb}),
        (ra, lambda j: {"row": ((r // rb + j) % ra) * rb + r % rb, "col": c}),
        (ca, lambda j: {"row": r, "col": ((c // cb + j) % ca) * cb + c % cb}),
    ):
        groups.append([(j, place(j)) for j in range(1, size)])

    for k in range(9):
        for p in range(n_pos):
            for d in range(2):
                if k == 4:
                    noff[k, p, d] = off[0, 0, p, d]
                else:
                    noff[k, p, d] = 4096

    for k in range(2):
        for cond, place in (
            (jnp.logical_not(has_outer), (slice(None), pl.ds(outer, HALO))),
            (c == 0, (0, pl.ds(0, 512))),
            (c == n_col - 1, (3, pl.ds(0, 512))),
        ):
            @pl.when(cond)
            def _(k=k, place=place):
                ref = spans[k].at[(slice(None),) + place + (slice(None),)]
                ref[...] = jnp.zeros(ref.shape, f32)

    barrier = pltpu.get_barrier_semaphore()
    total = 0
    for dr, dc in NEIGHBOURS:
        here = exists(dr, dc)
        total = total + here.astype(jnp.int32)

        @pl.when(here)
        def _(dr=dr, dc=dc):
            pl.semaphore_signal(barrier, inc=1, device_id={"row": r + dr, "col": c + dc}, device_id_type=MESH)

    for group in groups:
        for j, place in group:
            pl.semaphore_signal(barrier, inc=1, device_id=place, device_id_type=MESH)
            total = total + 1

    copies = [
        pltpu.make_async_copy(spec.at[:, :, pl.ds(0, HALF)], span_a.at[:, 1, pl.ds(HALO, WIN), :], local_sem.at[0]),
        pltpu.make_async_copy(spec.at[:, :, pl.ds(HALF, HALF)], span_a.at[:, 2, pl.ds(HALO, WIN), :], local_sem.at[1]),
        pltpu.make_async_copy(probe_in, probe, local_sem.at[2]),
        pltpu.make_async_copy(tab_in, tab, local_sem.at[3]),
        pltpu.make_async_copy(amp_in.at[0, 0], amp, local_sem.at[4]),
    ]
    for copy in copies:
        copy.start()
    copies[0].wait()
    copies[1].wait()

    pl.semaphore_wait(barrier, total)

    def along(dc, src, dst, cond=None):
        send_if, recv_if = col_ok(c + dc), col_ok(c - dc)
        if cond is not None:
            send_if, recv_if = send_if & cond(c), recv_if & cond(c - dc)
        return Message(pool, {"row": r, "col": c + dc}, send_if, recv_if, src, dst)

    def strip(dc, src, dst, start, count, relay, also=None):
        edge = Z_LEN - 1 if dc > 0 else 0
        one, two = dc - dc * Z_LEN, dc * Z_LEN
        both = lambda f: f if also is None else (lambda x: f(x) & also)
        inside = both(lambda x: x % Z_LEN != edge)
        cross = both(lambda x: (x % Z_LEN == edge) & col_ok(x + dc))
        rows = pl.ds(start, count)
        whole = along(dc, src.at[:, rows, :], dst.at[:, rows, :], inside)
        pairs = []
        size = count // CHUNKS
        for n in range(CHUNKS):
            rows = pl.ds(start + n * size, size)
            slot = relay.at[:, pl.ds(n * size, size), :]
            pairs.append(
                (
                    along(one, src.at[:, rows, :], slot, cross),
                    along(two, slot, dst.at[:, rows, :], lambda x: cross(x - one)),
                )
            )
        return whole, pairs

    def widen(k):
        span = spans[k]
        relays, direct, far_strips, rows_in, corners, corner_relays, cores = [], [], [], [], [], [], []
        for i, (dc, here, there) in enumerate(((1, 2, 0), (-1, 1, 3))):
            whole, pairs = strip(dc, span.at[:, here], span.at[:, there], far, HALF, relay_strip.at[k, i])
            far_strips.append(whole)
            relays += pairs
            direct.append(
                along(dc, span.at[:, here, pl.ds(near, HALF), :], span.at[:, there, pl.ds(near, HALF), :])
            )
            rows = pl.ds(outer, HALF // 2)
            corners.append(
                along(dc, span.at[:, here, rows, :], span.at[:, there, rows, :], lambda x: has_outer)
            )
            whole, pairs = strip(
                dc, span.at[:, here], span.at[:, there], outer + HALF // 2, HALF // 2, relay_corner.at[k, i], has_outer
            )
            corners.append(whole)
            corner_relays += pairs
        mirrored_inner = (HALO + WIN) * odd
        for t in (0, 3):
            cores.append(
                Message(
                    pool, partner, None, None,
                    span.at[:, t, pl.ds(near, HALF), :],
                    span.at[:, t, pl.ds(pl.multiple_of(mirrored_inner, HALF), HALF), :],
                )
            )
        both_tiles = pl.ds(1, 2)
        rows_in.append(
            Message(
                pool, beyond, has_outer, has_outer,
                span.at[:, both_tiles, pl.ds(far, HALF), :],
                span.at[:, both_tiles, pl.ds(pl.multiple_of((HALO + WIN) * (1 - odd), HALF), HALF), :],
            )
        )
        rows_in.append(
            Message(
                pool, partner, None, None,
                span.at[:, both_tiles, pl.ds(near, HALF), :],
                span.at[:, both_tiles, pl.ds(pl.multiple_of(mirrored_inner, HALF), HALF), :],
            )
        )
        for first, _ in relays:
            first.start()
        for m in rows_in + direct + far_strips:
            m.start()

        def middle():
            for first, second in relays:
                first.recv()
                second.start()
            for m in rows_in:
                m.recv()
            for first, _ in corner_relays:
                first.start()
            for m in corners:
                m.start()
            for m in direct:
                m.recv()
            for m in cores:
                m.start()
            for first, second in corner_relays:
                first.recv()
                second.start()

        def end():
            for m in far_strips + cores + corners:
                m.recv()
            for _, second in relays + corner_relays:
                second.recv()
            for m in rows_in + direct + far_strips + cores + corners:
                m.sent()
            for first, second in relays + corner_relays:
                first.sent()
                second.sent()

        return middle, end

    middle, end = widen(0)
    off_copies = []
    for i, (dr, dc) in enumerate(NEIGHBOURS):
        slot = (-dr + 1) * 3 + (-dc + 1)
        copy = pltpu.make_async_remote_copy(
            off.at[0, 0], noff.at[slot], off_sem.at[0, i], off_sem.at[1, i],
            device_id={"row": r + dr, "col": c + dc}, device_id_type=MESH,
        )
        pl.when(exists(dr, dc))(copy.start)
        off_copies.append((copy, dr, dc))

    def clear(ref, count):
        def body(i, _):
            ref[i] = jnp.zeros(ref.shape[1:], f32)
            return 0

        lax.fori_loop(0, count, body, 0)

    clear(pad, 7)
    copies[2].wait()
    for t in range(2):
        cols = pl.ds(t * HALF, HALF)
        pad[2 + t, pl.ds(WIN, WIN), :] = probe[0, :, cols] * probe[0, :, cols] + probe[1, :, cols] * probe[1, :, cols]

    def clear_wide(i, _):
        p, rest = i // 12, i % 12
        wide[p, rest // 6, rest % 6] = jnp.zeros((3 * WIN, HALF), f32)
        return 0

    lax.fori_loop(0, n_pos * 12, clear_wide, 0)

    middle()

    for copy, dr, dc in off_copies:
        pl.when(exists(dr, dc))(copy.wait_send)
        pl.when(exists(-dr, -dc))(copy.wait_recv)

    light[...] = jnp.zeros(light.shape, f32)

    def add_light(i, _):
        tile, p = i // n_pos, i % n_pos
        top = jnp.clip(noff[tile, p, 0] + (tile // 3 - 1) * WIN, -WIN, WIN)
        side = jnp.clip(noff[tile, p, 1] + (tile % 3 - 1) * WIN, -WIN, WIN)
        rows = pl.ds(WIN - top, WIN)
        start_col = WIN - side
        q, s = start_col // HALF, start_col % HALF
        turn = (HALF - s) % HALF
        rolled = [pltpu.roll(pad[q + j, rows, :], turn, 1) for j in range(3)]
        keep = lane < HALF - s
        for t in range(2):
            light[t] = light[t] + jnp.where(keep, rolled[t], rolled[t + 1])
        return 0

    lax.fori_loop(0, 9 * n_pos, add_light, 0)

    peak = jnp.max(light[...].reshape(2 * WIN // 8, 8, HALF), axis=0)

    def peak_start(phase, value):
        peak_out[phase] = value
        items = []
        for j, place in groups[phase]:
            copy = pltpu.make_async_remote_copy(
                peak_out.at[phase], peak_in.at[phase, j], peak_send.at[phase, j], peak_recv.at[phase, j],
                device_id=place, device_id_type=MESH,
            )
            copy.start()
            items.append(copy)
        return items

    def peak_finish(phase, items):
        for copy in items:
            copy.wait()
        value = peak_out[phase]
        for j, _ in groups[phase]:
            value = jnp.maximum(value, peak_in[phase, j])
        return value

    items = peak_start(0, peak)

    copies[3].wait()
    copies[4].wait()

    def order_amp(p, _):
        rows = tab[8]
        high, low = split(amp[p])
        x = dot(jnp.concatenate([rows, rows], axis=1), jnp.concatenate([high, low], axis=0))
        high, low = split(x)
        cols = tab[9]
        amp[p] = dot(jnp.concatenate([high, low], axis=1), jnp.concatenate([cols, cols], axis=0))
        return 0

    lax.fori_loop(0, n_pos, order_amp, 0)
    peak = peak_finish(0, items)
    items = peak_start(1, peak)

    end()

    def cat(a, b, axis):
        return jnp.concatenate([a, b], axis=axis)

    def window(k, p):
        top = off[0, 0, p, 0] + HALO
        side = off[0, 0, p, 1] + HALO
        q, s = side // HALF, side % HALF
        rows = pl.ds(top, WIN)
        turn = (HALF - s) % HALF
        keep = lane < HALF - s
        patch = []
        for part in range(2):
            rolled = [
                pltpu.roll(spans[k][part, jnp.minimum(q + j, 3), rows, :], turn, 1) for j in range(3)
            ]
            patch.append(cat(jnp.where(keep, rolled[0], rolled[1]), jnp.where(keep, rolled[1], rolled[2]), 1))
        pr, pi = probe[0], probe[1]
        er = pr * patch[0] - pi * patch[1]
        ei = pr * patch[1] + pi * patch[0]
        sums = cat(er[:HALF] + er[HALF:], ei[:HALF] + ei[HALF:], 0)
        difs = cat(er[:HALF] - er[HALF:], ei[:HALF] - ei[HALF:], 0)
        even = left(tab, 0, sums)
        odd = left(tab, 1, difs)
        xr = cat(even[:HALF], odd[:HALF], 0)
        xi = cat(even[HALF:], odd[HALF:], 0)
        sums = cat(xr[:, :HALF] + xr[:, HALF:], xi[:, :HALF] + xi[:, HALF:], 1)
        difs = cat(xr[:, :HALF] - xr[:, HALF:], xi[:, :HALF] - xi[:, HALF:], 1)
        out_cols = []
        for index, x in ((0, sums), (1, difs)):
            far = right(x, tab, 2 + index)
            fr, fi = far[:, :HALF], far[:, HALF:]
            factor = 1.0 - amp[p, :, pl.ds(index * HALF, HALF)] * lax.rsqrt(fr * fr + fi * fi + SMOOTH)
            out_cols.append(right(cat(factor * fr, factor * fi, 1), tab, index))
        lo, hi = out_cols[0] + out_cols[1], out_cols[0] - out_cols[1]
        xr = cat(lo[:, :HALF], hi[:, :HALF], 1)
        xi = cat(lo[:, HALF:], hi[:, HALF:], 1)
        even = left(tab, 2, cat(xr[:HALF], xi[:HALF], 0))
        odd = left(tab, 3, cat(xr[HALF:], xi[HALF:], 0))
        lo, hi = even + odd, even - odd
        br = cat(lo[:HALF], hi[:HALF], 0)
        bi = cat(lo[HALF:], hi[HALF:], 0)
        g = (pr * br + pi * bi, pr * bi - pi * br)
        past = lane >= s
        zero = jnp.zeros((WIN, HALF), f32)
        for part in range(2):
            one = pltpu.roll(g[part][:, :HALF], s, 1)
            two = pltpu.roll(g[part][:, HALF:], s, 1)
            wide[p, part, 2, pl.ds(WIN, WIN), :] = jnp.where(past, one, zero)
            wide[p, part, 3, pl.ds(WIN, WIN), :] = jnp.where(past, two, one)
            wide[p, part, 4, pl.ds(WIN, WIN), :] = jnp.where(past, zero, two)

    tops = [off[0, 0, p, 0] + HALO for p in range(n_pos)]
    tiles = [(off[0, 0, p, 1] + HALO) // HALF for p in range(n_pos)]

    def gather(k, t, start):
        for part in range(2):
            acc = None
            for p in range(n_pos):
                piece = wide[p, part, 2 + t - tiles[p], pl.ds(WIN - tops[p] + start, HALF), :]
                acc = piece if acc is None else acc + piece
            grad[k, part, t, pl.ds(start, HALF), :] = acc

    def accumulate(k, t, start, ref):
        for part in range(2):
            rows = pl.ds(start, HALF)
            grad[k, part, t, rows, :] = grad[k, part, t, rows, :] + ref[part]

    def fold(k, between):
        g = grad.at[k]
        relays, direct, far_strips, corners, corner_relays, cores = [], [], [], [], [], []
        for i, (dc, here) in enumerate(((1, 3), (-1, 0))):
            whole, pairs = strip(dc, g.at[:, here], col_in.at[k, i], far, HALF, relay_strip.at[ITERS + k, i])
            far_strips.append(whole)
            relays += pairs
            direct.append(
                along(dc, g.at[:, here, pl.ds(near, HALF), :], col_in.at[k, i, :, pl.ds(near, HALF), :])
            )
            rows = pl.ds(outer, HALF // 2)
            corners.append(
                along(dc, g.at[:, here, rows, :], corner_in.at[k, i, :, rows, :], lambda x: has_outer)
            )
            whole, pairs = strip(
                dc, g.at[:, here], corner_in.at[k, i], outer + HALF // 2, HALF // 2,
                relay_corner.at[ITERS + k, i], has_outer,
            )
            corners.append(whole)
            corner_relays += pairs
            cores.append(
                Message(pool, partner, None, None, g.at[:, here, pl.ds(inner, HALF), :], core_in.at[k, i])
            )
        both_tiles = pl.ds(1, 2)
        row_out = Message(
            pool, beyond, has_outer, has_outer, g.at[:, both_tiles, pl.ds(outer, HALF), :], row_in.at[k, 0]
        )
        row_core = Message(pool, partner, None, None, g.at[:, both_tiles, pl.ds(inner, HALF), :], row_in.at[k, 1])

        for t in (0, 3):
            gather(k, t, outer)
        for first, _ in corner_relays:
            first.start()
        for m in corners:
            m.start()
        for t in (0, 3):
            gather(k, t, inner)
        for m in cores:
            m.start()
        for t in (0, 3):
            gather(k, t, far)
        for first, _ in relays:
            first.start()
        for m in far_strips:
            m.start()
        for t in (0, 3):
            gather(k, t, near)
        for t in (1, 2):
            gather(k, t, outer)
        for i, m in enumerate(cores):
            m.recv()
            accumulate(k, (3, 0)[i], near, core_in.at[k, i])
        for m in direct:
            m.start()
        for first, second in corner_relays:
            first.recv()
            second.start()
        for t in (1, 2):
            gather(k, t, inner)
        row_core.start()
        for first, second in relays:
            first.recv()
            second.start()
        for m in corners:
            m.recv()
        for _, second in corner_relays:
            second.recv()
        for i in range(2):
            @pl.when(has_outer & col_ok(c - (1, -1)[i]))
            def _(i=i):
                accumulate(k, 1 + i, outer, corner_in.at[k, i, :, pl.ds(outer, HALF), :])
        row_out.start()
        for t in (1, 2):
            gather(k, t, near)
            gather(k, t, far)
        between()
        row_core.recv()
        for t in (1, 2):
            accumulate(k, t, near, row_in.at[k, 1, :, t - 1])
        for m in direct + far_strips:
            m.recv()
        for _, second in relays:
            second.recv()
        for i in range(2):
            @pl.when(col_ok(c - (1, -1)[i]))
            def _(i=i):
                for start in (near, far):
                    accumulate(k, 1 + i, start, col_in.at[k, i, :, pl.ds(start, HALF), :])
        row_out.recv()

        @pl.when(has_outer)
        def _():
            for t in (1, 2):
                accumulate(k, t, far, row_in.at[k, 0, :, t - 1])

        def end():
            for m in [row_out, row_core] + direct + far_strips + corners + cores:
                m.sent()
            for first, second in relays + corner_relays:
                first.sent()
                second.sent()

        return end

    for k in range(ITERS):
        lax.fori_loop(0, n_pos, lambda p, _, k=k: (window(k, p), 0)[1], 0)

        def between():
            if k == 0:
                value = peak_finish(1, items)
                value = peak_finish(2, peak_start(2, value))
                value = jnp.max(peak_finish(3, peak_start(3, value)))
                inv[...] = 1.0 / (light[...] + RIDGE * value)

        end = fold(k, between)
        for t in range(2):
            for part in range(2):
                new = spans[k][part, 1 + t, pl.ds(HALO, WIN), :] - grad[k, part, 1 + t, pl.ds(HALO, WIN), :] * inv[t]
                if k + 1 < ITERS:
                    spans[k + 1][part, 1 + t, pl.ds(HALO, WIN), :] = new
                else:
                    out[part, :, pl.ds(t * HALF, HALF)] = new
        if k + 1 < ITERS:
            middle, end_widen = widen(k + 1)
            middle()
            end_widen()
        end()


def solution(mesh):
    n_row, n_col = mesh.shape["row"], mesh.shape["col"]
    tables = dft_tables()

    def local(specimen, probe_field, offsets, amplitudes):
        n_pos = offsets.shape[2]
        vmem = lambda *shape: pltpu.VMEM(shape, jnp.float32)
        dma = lambda *shape: pltpu.SemaphoreType.DMA(shape)
        return pl.pallas_call(
            functools.partial(kernel, n_row, n_col, n_pos),
            out_shape=jax.ShapeDtypeStruct((2, WIN, WIN), jnp.float32),
            in_specs=[
                pl.BlockSpec(memory_space=pl.ANY),
                pl.BlockSpec(memory_space=pl.ANY),
                pl.BlockSpec(memory_space=pltpu.SMEM),
                pl.BlockSpec(memory_space=pl.ANY),
                pl.BlockSpec(memory_space=pl.ANY),
            ],
            out_specs=pl.BlockSpec(memory_space=pltpu.VMEM),
            scratch_shapes=[
                vmem(2, 4, 512, HALF),
                vmem(2, 4, 512, HALF),
                vmem(ITERS, 2, 4, 512, HALF),
                vmem(n_pos, 2, 6, 3 * WIN, HALF),
                vmem(7, 3 * WIN, HALF),
                vmem(2, WIN, HALF),
                vmem(2, WIN, HALF),
                vmem(2, WIN, WIN),
                vmem(n_pos, WIN, WIN),
                pltpu.VMEM((10, WIN, WIN), jnp.bfloat16),
                pltpu.SMEM((9, n_pos, 2), jnp.int32),
                vmem(ITERS, 2, 2, 512, HALF),
                vmem(ITERS, 2, 2, HALF, HALF),
                vmem(ITERS, 2, 2, 2, HALO, HALF),
                vmem(ITERS, 2, 2, 512, HALF),
                vmem(2 * ITERS, 2, 2, HALF, HALF),
                vmem(2 * ITERS, 2, 2, HALF // 2, HALF),
                vmem(4, 8, HALF),
                vmem(4, 8, 8, HALF),
                dma(5),
                dma(2, 8),
                dma(112),
                dma(112),
                dma(4, 8),
                dma(4, 8),
            ],
            compiler_params=pltpu.CompilerParams(
                collective_id=0, has_side_effects=True, vmem_limit_bytes=56 * 1024 * 1024
            ),
        )(specimen, probe_field, offsets, amplitudes, jnp.asarray(tables))

    return jax.shard_map(
        local,
        mesh=mesh,
        in_specs=(
            P(None, "row", "col"),
            P(),
            P("row", "col", None, None),
            P("row", "col", None, None, None),
        ),
        out_specs=P(None, "row", "col"),
        check_vma=False,
    )
```

```python
import functools
import math

import jax
import jax.numpy as jnp
import ml_dtypes
import numpy as np
from jax import lax
from jax.experimental import pallas as pl
from jax.experimental.pallas import tpu as pltpu
from jax.sharding import PartitionSpec as P

WIN = 256
HALF = 128
HALO = 128
ITERS = 2
SMOOTH = 0.25
RIDGE = 0.1
MESH = pl.DeviceIdType.MESH

NEIGHBOURS = [(a, b) for a in (-1, 0, 1) for b in (-1, 0, 1) if (a, b) != (0, 0)]


def dft_tables():
    n = np.arange(HALF)[None, :]
    m = np.arange(HALF)[:, None]
    blocks = []
    for freq in (2 * m, 2 * m + 1):
        angle = -2.0 * math.pi * ((freq * n) % WIN) / WIN
        re, im = np.cos(angle) / 16.0, np.sin(angle) / 16.0
        blocks.append(np.block([[re, -im], [im, re]]))
    out = []
    for block in (blocks[0], blocks[1], blocks[0].T, blocks[1].T):
        high = block.astype(ml_dtypes.bfloat16)
        low = (block - high.astype(np.float64)).astype(ml_dtypes.bfloat16)
        out += [high, low]
    order = np.concatenate([np.arange(0, WIN, 2), np.arange(1, WIN, 2)])
    perm = (order[:, None] == np.arange(WIN)[None, :]).astype(ml_dtypes.bfloat16)
    out += [perm, perm.T]
    return np.stack(out)


def split(x):
    high = x.astype(jnp.bfloat16)
    low = (x - high.astype(jnp.float32)).astype(jnp.bfloat16)
    return high, low


def dot(a, b):
    return jnp.dot(a, b, preferred_element_type=jnp.float32)


def left(tab, index, x):
    high, low = split(x)
    th, tl = tab[2 * index], tab[2 * index + 1]
    return dot(jnp.concatenate([th, th, tl], axis=1), jnp.concatenate([high, low, high], axis=0))


def right(x, tab, index):
    high, low = split(x)
    th, tl = tab[2 * index], tab[2 * index + 1]
    return dot(jnp.concatenate([high, low, high], axis=1), jnp.concatenate([th, th, tl], axis=0))


def digits(size, part):
    return (size // part, part) if size > part else (1, size)


Z_LEN = 8
CHUNKS = 2


class Message:
    def __init__(self, pool, device, send_if, recv_if, src, dst):
        send, recv, index = pool[0], pool[1], pool[2]
        pool[2] += 1
        self.send_if, self.recv_if = send_if, recv_if
        self.copy = pltpu.make_async_remote_copy(
            src, dst, send.at[index], recv.at[index], device_id=device, device_id_type=MESH
        )

    def _when(self, cond, action):
        if cond is None:
            action()
        else:
            pl.when(cond)(action)

    def start(self):
        self._when(self.send_if, self.copy.start)

    def recv(self):
        self._when(self.recv_if, self.copy.wait_recv)

    def sent(self):
        self._when(self.send_if, self.copy.wait_send)


def kernel(
    n_row, n_col, n_pos,
    spec, probe_in, off, amp_in, tab_in,
    out,
    span_a, span_b, grad, wide, pad, light, inv, probe, amp, tab, noff,
    corner_in, core_in, row_in, col_in, relay_strip, relay_row, peak_out, peak_in,
    local_sem, off_sem, send_sem, recv_sem, peak_send, peak_recv,
):
    r, c = lax.axis_index("row"), lax.axis_index("col")
    f32 = jnp.float32
    spans = (span_a, span_b)
    lane = lax.broadcasted_iota(jnp.int32, (1, HALF), 1)
    pool = [send_sem, recv_sem, 0]

    odd = r % 2
    near = pl.multiple_of(HALO + HALF - HALF * odd, HALF)
    far = pl.multiple_of(HALO + HALF * odd, HALF)
    inner = pl.multiple_of((HALO + WIN) * (1 - odd), HALF)
    outer = pl.multiple_of((HALO + WIN) * odd, HALF)
    inner_there, outer_there = outer, inner
    partner = {"row": r + 1 - 2 * odd, "col": c}
    r_out = r - 1 + 2 * odd
    has_outer = (r_out >= 0) & (r_out < n_row)
    beyond = {"row": r_out, "col": c}

    def exists(dr, dc):
        ok = None
        for index, step, size in ((r, dr, n_row), (c, dc, n_col)):
            if step:
                here = (index + step >= 0) & (index + step < size)
                ok = here if ok is None else ok & here
        return ok

    def col_ok(x):
        return (x >= 0) & (x < n_col)

    ra, rb = digits(n_row, 4)
    ca, cb = digits(n_col, Z_LEN)
    groups = []
    for size, place in (
        (rb, lambda j: {"row": (r // rb) * rb + (r % rb + j) % rb, "col": c}),
        (cb, lambda j: {"row": r, "col": (c // cb) * cb + (c % cb + j) % cb}),
        (ra, lambda j: {"row": ((r // rb + j) % ra) * rb + r % rb, "col": c}),
        (ca, lambda j: {"row": r, "col": ((c // cb + j) % ca) * cb + c % cb}),
    ):
        groups.append([(j, place(j)) for j in range(1, size)])

    for k in range(9):
        for p in range(n_pos):
            for d in range(2):
                if k == 4:
                    noff[k, d, p] = off[0, 0, d, p]
                else:
                    noff[k, d, p] = 4096

    for k in range(2):
        for cond, place in (
            (jnp.logical_not(has_outer), (slice(None), pl.ds(outer, HALO))),
            (c == 0, (0, pl.ds(0, 512))),
            (c == n_col - 1, (3, pl.ds(0, 512))),
        ):
            @pl.when(cond)
            def _(k=k, place=place):
                ref = spans[k].at[(slice(None),) + place + (slice(None),)]
                ref[...] = jnp.zeros(ref.shape, f32)

    barrier = pltpu.get_barrier_semaphore()
    total = 0
    for dr, dc in NEIGHBOURS:
        here = exists(dr, dc)
        total = total + here.astype(jnp.int32)

        @pl.when(here)
        def _(dr=dr, dc=dc):
            pl.semaphore_signal(barrier, inc=1, device_id={"row": r + dr, "col": c + dc}, device_id_type=MESH)

    for group in groups:
        for j, place in group:
            pl.semaphore_signal(barrier, inc=1, device_id=place, device_id_type=MESH)
            total = total + 1

    copies = [
        pltpu.make_async_copy(spec.at[:, :, pl.ds(0, HALF)], span_a.at[:, 1, pl.ds(HALO, WIN), :], local_sem.at[0]),
        pltpu.make_async_copy(spec.at[:, :, pl.ds(HALF, HALF)], span_a.at[:, 2, pl.ds(HALO, WIN), :], local_sem.at[1]),
        pltpu.make_async_copy(probe_in, probe, local_sem.at[2]),
        pltpu.make_async_copy(tab_in, tab, local_sem.at[3]),
        pltpu.make_async_copy(amp_in.at[0, 0], amp, local_sem.at[4]),
    ]
    for copy in copies:
        copy.start()
    copies[0].wait()
    copies[1].wait()

    pl.semaphore_wait(barrier, total)

    def along(dc, src, dst, cond=None):
        send_if, recv_if = col_ok(c + dc), col_ok(c - dc)
        if cond is not None:
            send_if, recv_if = send_if & cond(c), recv_if & cond(c - dc)
        return Message(pool, {"row": r, "col": c + dc}, send_if, recv_if, src, dst)

    def strip(dc, src, dst, start, count, relay, also=None):
        edge = Z_LEN - 1 if dc > 0 else 0
        one, two = dc - dc * Z_LEN, dc * Z_LEN
        both = lambda f: f if also is None else (lambda x: f(x) & also)
        inside = both(lambda x: x % Z_LEN != edge)
        cross = both(lambda x: (x % Z_LEN == edge) & col_ok(x + dc))
        rows = pl.ds(start, count)
        whole = along(dc, src.at[:, rows, :], dst.at[:, rows, :], inside)
        pairs = []
        size = count // CHUNKS
        for n in range(CHUNKS):
            rows = pl.ds(start + n * size, size)
            slot = relay.at[:, pl.ds(n * size, size), :]
            pairs.append(
                (
                    along(one, src.at[:, rows, :], slot, cross),
                    along(two, slot, dst.at[:, rows, :], lambda x: cross(x - one)),
                )
            )
        return whole, pairs

    def planes(x):
        return ((x % Z_LEN == Z_LEN - 1) & (x < n_col - 1)) | ((x % Z_LEN == 0) & (x > 0))

    def outer_rows(src, dst, relay):
        half, size = HALF // 2, HALF // 2 // CHUNKS
        end_here = planes(c)
        first_end = c % Z_LEN == 0
        passes = ((c % Z_LEN == Z_LEN - 2) & planes(c + 1)) | ((c % Z_LEN == 1) & planes(c - 1))
        to_relay = {"row": r, "col": c + jnp.where(first_end, 1, -1)}
        from_relay = {"row": r_out, "col": c + jnp.where(c % Z_LEN == 1, -1, 1)}

        def part(start, count, cond):
            rows = pl.ds(start, count)
            return Message(pool, beyond, cond, cond, src.at[:, :, rows, :], dst.at[:, :, rows, :])

        direct = [part(0, half, has_outer), part(half, half, has_outer & jnp.logical_not(end_here))]
        pairs = []
        for n in range(CHUNKS):
            rows = pl.ds(half + n * size, size)
            slot = relay.at[:, :, pl.ds(n * size, size), :]
            pairs.append(
                (
                    Message(pool, to_relay, has_outer & end_here, has_outer & passes, src.at[:, :, rows, :], slot),
                    Message(pool, from_relay, has_outer & passes, has_outer & end_here, slot, dst.at[:, :, rows, :]),
                )
            )
        return direct, pairs

    both_tiles = pl.ds(1, 2)

    def widen(k):
        span = spans[k]
        relays, direct, far_strips, corners, cores = [], [], [], [], []
        for i, (dc, here, there) in enumerate(((1, 2, 0), (-1, 1, 3))):
            whole, pairs = strip(dc, span.at[:, here], span.at[:, there], far, HALF, relay_strip.at[k, i])
            far_strips.append(whole)
            relays += pairs
            direct.append(
                along(dc, span.at[:, here, pl.ds(near, HALF), :], span.at[:, there, pl.ds(near, HALF), :])
            )
            rows = pl.ds(outer, HALF)
            corners.append(
                along(dc, span.at[:, here, rows, :], span.at[:, there, rows, :], lambda x: has_outer)
            )
        mirrored = pl.ds(inner_there, HALF)
        for t in (0, 3):
            cores.append(
                Message(
                    pool, partner, None, None, span.at[:, t, pl.ds(near, HALF), :], span.at[:, t, mirrored, :]
                )
            )
        row_core = Message(
            pool, partner, None, None,
            span.at[:, both_tiles, pl.ds(near, HALF), :], span.at[:, both_tiles, mirrored, :],
        )
        row_far, row_relays = outer_rows(
            span.at[:, both_tiles, pl.ds(far, HALF), :],
            span.at[:, both_tiles, pl.ds(outer_there, HALF), :],
            relay_row.at[k],
        )

        def start_far():
            for first, _ in relays + row_relays:
                first.start()
            for m in row_far + far_strips:
                m.start()

        def start_near():
            row_core.start()
            for m in direct:
                m.start()

        def relay(n):
            for pairs in (relays, row_relays):
                for first, second in pairs[n::CHUNKS]:
                    first.recv()
                    second.start()

        def middle():
            for m in row_far:
                m.recv()
            for _, second in row_relays:
                second.recv()
            row_core.recv()
            for m in corners:
                m.start()
            for m in direct:
                m.recv()
            for m in cores:
                m.start()

        def end():
            for m in far_strips + cores + corners:
                m.recv()
            for _, second in relays:
                second.recv()
            for m in [row_core] + row_far + direct + far_strips + cores + corners:
                m.sent()
            for first, second in relays + row_relays:
                first.sent()
                second.sent()

        return start_near, start_far, relay, middle, end

    start_near, start_far, relay, middle, end = widen(0)
    off_copies = []
    for i, (dr, dc) in enumerate(NEIGHBOURS):
        slot = (-dr + 1) * 3 + (-dc + 1)
        copy = pltpu.make_async_remote_copy(
            off.at[0, 0], noff.at[slot], off_sem.at[0, i], off_sem.at[1, i],
            device_id={"row": r + dr, "col": c + dc}, device_id_type=MESH,
        )
        pl.when(exists(dr, dc))(copy.start)
        off_copies.append((copy, dr, dc))
    start_far()
    start_near()

    def clear(ref, count):
        def body(i, _):
            ref[i] = jnp.zeros(ref.shape[1:], f32)
            return 0

        lax.fori_loop(0, count, body, 0)

    clear(pad, 7)
    copies[2].wait()
    for t in range(2):
        cols = pl.ds(t * HALF, HALF)
        pad[2 + t, pl.ds(WIN, WIN), :] = probe[0, :, cols] * probe[0, :, cols] + probe[1, :, cols] * probe[1, :, cols]

    def clear_wide(i, _):
        p, rest = i // 12, i % 12
        wide[p, rest // 6, rest % 6] = jnp.zeros((3 * WIN, HALF), f32)
        return 0

    for copy, dr, dc in off_copies:
        pl.when(exists(dr, dc))(copy.wait_send)
        pl.when(exists(-dr, -dc))(copy.wait_recv)

    light[...] = jnp.zeros(light.shape, f32)

    def add_light(i, _):
        tile, p = i // n_pos, i % n_pos
        top = jnp.clip(noff[tile, 0, p] + (tile // 3 - 1) * WIN, -WIN, WIN)
        side = jnp.clip(noff[tile, 1, p] + (tile % 3 - 1) * WIN, -WIN, WIN)
        rows = pl.ds(WIN - top, WIN)
        start_col = WIN - side
        q, s = start_col // HALF, start_col % HALF
        turn = (HALF - s) % HALF
        rolled = [pltpu.roll(pad[q + j, rows, :], turn, 1) for j in range(3)]
        keep = lane < HALF - s
        for t in range(2):
            light[t] = light[t] + jnp.where(keep, rolled[t], rolled[t + 1])
        return 0

    for n in range(3):
        lax.fori_loop(3 * n * n_pos, 3 * (n + 1) * n_pos, add_light, 0)
        if n < CHUNKS:
            relay(n)

    peak = jnp.max(light[...].reshape(2 * WIN // 8, 8, HALF), axis=0)

    def peak_start(phase, value):
        peak_out[phase] = value
        items = []
        for j, place in groups[phase]:
            copy = pltpu.make_async_remote_copy(
                peak_out.at[phase], peak_in.at[phase, j], peak_send.at[phase, j], peak_recv.at[phase, j],
                device_id=place, device_id_type=MESH,
            )
            copy.start()
            items.append(copy)
        return items

    def peak_finish(phase, items):
        for copy in items:
            copy.wait()
        value = peak_out[phase]
        for j, _ in groups[phase]:
            value = jnp.maximum(value, peak_in[phase, j])
        return value

    items = peak_start(0, peak)
    middle()

    lax.fori_loop(0, n_pos * 12, clear_wide, 0)

    copies[3].wait()
    copies[4].wait()

    def order_amp(p, _):
        rows = tab[8]
        high, low = split(amp[p])
        x = dot(jnp.concatenate([rows, rows], axis=1), jnp.concatenate([high, low], axis=0))
        high, low = split(x)
        cols = tab[9]
        amp[p] = dot(jnp.concatenate([high, low], axis=1), jnp.concatenate([cols, cols], axis=0))
        return 0

    lax.fori_loop(0, n_pos, order_amp, 0)
    peak = peak_finish(0, items)
    items = peak_start(1, peak)
    end()

    def cat(a, b, axis):
        return jnp.concatenate([a, b], axis=axis)

    def window(k, p):
        top = off[0, 0, 0, p] + HALO
        side = off[0, 0, 1, p] + HALO
        q, s = side // HALF, side % HALF
        rows = pl.ds(top, WIN)
        turn = (HALF - s) % HALF
        keep = lane < HALF - s
        patch = []
        for part in range(2):
            rolled = [
                pltpu.roll(spans[k][part, jnp.minimum(q + j, 3), rows, :], turn, 1) for j in range(3)
            ]
            patch.append(cat(jnp.where(keep, rolled[0], rolled[1]), jnp.where(keep, rolled[1], rolled[2]), 1))
        pr, pi = probe[0], probe[1]
        er = pr * patch[0] - pi * patch[1]
        ei = pr * patch[1] + pi * patch[0]
        sums = cat(er[:HALF] + er[HALF:], ei[:HALF] + ei[HALF:], 0)
        difs = cat(er[:HALF] - er[HALF:], ei[:HALF] - ei[HALF:], 0)
        even = left(tab, 0, sums)
        odd = left(tab, 1, difs)
        xr = cat(even[:HALF], odd[:HALF], 0)
        xi = cat(even[HALF:], odd[HALF:], 0)
        sums = cat(xr[:, :HALF] + xr[:, HALF:], xi[:, :HALF] + xi[:, HALF:], 1)
        difs = cat(xr[:, :HALF] - xr[:, HALF:], xi[:, :HALF] - xi[:, HALF:], 1)
        out_cols = []
        for index, x in ((0, sums), (1, difs)):
            far = right(x, tab, 2 + index)
            fr, fi = far[:, :HALF], far[:, HALF:]
            factor = 1.0 - amp[p, :, pl.ds(index * HALF, HALF)] * lax.rsqrt(fr * fr + fi * fi + SMOOTH)
            out_cols.append(right(cat(factor * fr, factor * fi, 1), tab, index))
        lo, hi = out_cols[0] + out_cols[1], out_cols[0] - out_cols[1]
        xr = cat(lo[:, :HALF], hi[:, :HALF], 1)
        xi = cat(lo[:, HALF:], hi[:, HALF:], 1)
        even = left(tab, 2, cat(xr[:HALF], xi[:HALF], 0))
        odd = left(tab, 3, cat(xr[HALF:], xi[HALF:], 0))
        lo, hi = even + odd, even - odd
        br = cat(lo[:HALF], hi[:HALF], 0)
        bi = cat(lo[HALF:], hi[HALF:], 0)
        g = (pr * br + pi * bi, pr * bi - pi * br)
        past = lane >= s
        zero = jnp.zeros((WIN, HALF), f32)
        for part in range(2):
            one = pltpu.roll(g[part][:, :HALF], s, 1)
            two = pltpu.roll(g[part][:, HALF:], s, 1)
            wide[p, part, 2, pl.ds(WIN, WIN), :] = jnp.where(past, one, zero)
            wide[p, part, 3, pl.ds(WIN, WIN), :] = jnp.where(past, two, one)
            wide[p, part, 4, pl.ds(WIN, WIN), :] = jnp.where(past, zero, two)

    tops = [off[0, 0, 0, p] + HALO for p in range(n_pos)]
    tiles = [(off[0, 0, 1, p] + HALO) // HALF for p in range(n_pos)]

    def gather(k, t, start):
        for part in range(2):
            acc = None
            for p in range(n_pos):
                piece = wide[p, part, 2 + t - tiles[p], pl.ds(WIN - tops[p] + start, HALF), :]
                acc = piece if acc is None else acc + piece
            grad[k, part, t, pl.ds(start, HALF), :] = acc

    def accumulate(k, t, start, ref):
        for part in range(2):
            rows = pl.ds(start, HALF)
            grad[k, part, t, rows, :] = grad[k, part, t, rows, :] + ref[part]

    def fold(k, on_near, on_far):
        g = grad.at[k]
        relays, direct, far_strips, corners, cores = [], [], [], [], []
        for i, (dc, here) in enumerate(((1, 3), (-1, 0))):
            whole, pairs = strip(dc, g.at[:, here], col_in.at[k, i], far, HALF, relay_strip.at[ITERS + k, i])
            far_strips.append(whole)
            relays += pairs
            direct.append(
                along(dc, g.at[:, here, pl.ds(near, HALF), :], col_in.at[k, i, :, pl.ds(near, HALF), :])
            )
            corners.append(
                along(dc, g.at[:, here, pl.ds(outer, HALF), :], corner_in.at[k, i], lambda x: has_outer)
            )
            cores.append(
                Message(pool, partner, None, None, g.at[:, here, pl.ds(inner, HALF), :], core_in.at[k, i])
            )
        row_far, row_relays = outer_rows(
            g.at[:, both_tiles, pl.ds(outer, HALF), :], row_in.at[k, 0], relay_row.at[ITERS + k]
        )
        row_core = Message(pool, partner, None, None, g.at[:, both_tiles, pl.ds(inner, HALF), :], row_in.at[k, 1])

        for t in (0, 3):
            gather(k, t, outer)
        for m in corners:
            m.start()
        for t in (0, 3):
            gather(k, t, inner)
        for m in cores:
            m.start()
        for t in (0, 3):
            gather(k, t, far)
        for first, _ in relays:
            first.start()
        for m in far_strips:
            m.start()
        for t in (0, 3):
            gather(k, t, near)
        for t in (1, 2):
            gather(k, t, outer)
        for i, m in enumerate(cores):
            m.recv()
            accumulate(k, (3, 0)[i], near, core_in.at[k, i])
        for m in direct:
            m.start()
        for t in (1, 2):
            gather(k, t, inner)
        row_core.start()
        for i, m in enumerate(corners):
            m.recv()

            @pl.when(has_outer & col_ok(c - (1, -1)[i]))
            def _(i=i):
                accumulate(k, 1 + i, outer, corner_in.at[k, i])
        for first, _ in row_relays:
            first.start()
        for m in row_far:
            m.start()
        for first, second in relays:
            first.recv()
            second.start()
        for t in (1, 2):
            gather(k, t, near)
            gather(k, t, far)
        for first, second in row_relays:
            first.recv()
            second.start()
        row_core.recv()
        for t in (1, 2):
            accumulate(k, t, near, row_in.at[k, 1, :, t - 1])

        def columns(start):
            for i in range(2):
                @pl.when(col_ok(c - (1, -1)[i]))
                def _(i=i):
                    accumulate(k, 1 + i, start, col_in.at[k, i, :, pl.ds(start, HALF), :])

        for m in direct:
            m.recv()
        columns(near)
        on_near()
        for m in far_strips:
            m.recv()
        for _, second in relays:
            second.recv()
        columns(far)
        for m in row_far:
            m.recv()
        for _, second in row_relays:
            second.recv()

        @pl.when(has_outer)
        def _():
            for t in (1, 2):
                accumulate(k, t, far, row_in.at[k, 0, :, t - 1])

        on_far()

        def end():
            for m in [row_core] + row_far + direct + far_strips + corners + cores:
                m.sent()
            for first, second in relays + row_relays:
                first.sent()
                second.sent()

        return end

    def update(k, start):
        rows = pl.ds(start, HALF)
        for t in range(2):
            for part in range(2):
                step = grad[k, part, 1 + t, rows, :] * inv[t, pl.ds(start - HALO, HALF), :]
                new = spans[k][part, 1 + t, rows, :] - step
                if k + 1 < ITERS:
                    spans[k + 1][part, 1 + t, rows, :] = new
                else:
                    out[part, pl.ds(start - HALO, HALF), pl.ds(t * HALF, HALF)] = new

    for k in range(ITERS):
        last = k + 1 == ITERS
        for p in range(n_pos):
            window(k, p)
            if k == 0 and p < 3:
                peak = peak_finish(1 + p, items)
                if p < 2:
                    items = peak_start(2 + p, peak)
                else:
                    inv[...] = 1.0 / (light[...] + RIDGE * jnp.max(peak))
        if not last:
            start_near, start_far, relay, middle, end = widen(k + 1)

        def on_near():
            update(k, near)
            if not last:
                start_near()

        def on_far():
            update(k, far)
            if not last:
                start_far()

        end_fold = fold(k, on_near, on_far)
        if not last:
            for n in range(CHUNKS):
                relay(n)
            middle()
            end()
        end_fold()


def solution(mesh):
    n_row, n_col = mesh.shape["row"], mesh.shape["col"]
    tables = dft_tables()

    def local(specimen, probe_field, offsets, amplitudes):
        n_pos = offsets.shape[2]
        vmem = lambda *shape: pltpu.VMEM(shape, jnp.float32)
        dma = lambda *shape: pltpu.SemaphoreType.DMA(shape)
        return pl.pallas_call(
            functools.partial(kernel, n_row, n_col, n_pos),
            out_shape=jax.ShapeDtypeStruct((2, WIN, WIN), jnp.float32),
            in_specs=[
                pl.BlockSpec(memory_space=pl.ANY),
                pl.BlockSpec(memory_space=pl.ANY),
                pl.BlockSpec(memory_space=pltpu.SMEM),
                pl.BlockSpec(memory_space=pl.ANY),
                pl.BlockSpec(memory_space=pl.ANY),
            ],
            out_specs=pl.BlockSpec(memory_space=pltpu.VMEM),
            scratch_shapes=[
                vmem(2, 4, 512, HALF),
                vmem(2, 4, 512, HALF),
                vmem(ITERS, 2, 4, 512, HALF),
                vmem(n_pos, 2, 6, 3 * WIN, HALF),
                vmem(7, 3 * WIN, HALF),
                vmem(2, WIN, HALF),
                vmem(2, WIN, HALF),
                vmem(2, WIN, WIN),
                vmem(n_pos, WIN, WIN),
                pltpu.VMEM((10, WIN, WIN), jnp.bfloat16),
                pltpu.SMEM((9, 2, n_pos), jnp.int32),
                vmem(ITERS, 2, 2, HALF, HALF),
                vmem(ITERS, 2, 2, HALF, HALF),
                vmem(ITERS, 2, 2, 2, HALO, HALF),
                vmem(ITERS, 2, 2, 512, HALF),
                vmem(2 * ITERS, 2, 2, HALF, HALF),
                vmem(2 * ITERS, 2, 2, HALF // 2, HALF),
                vmem(4, 8, HALF),
                vmem(4, 8, 8, HALF),
                dma(5),
                dma(2, 8),
                dma(112),
                dma(112),
                dma(4, 8),
                dma(4, 8),
            ],
            compiler_params=pltpu.CompilerParams(
                collective_id=0, has_side_effects=True, vmem_limit_bytes=56 * 1024 * 1024
            ),
        )(specimen, probe_field, jnp.swapaxes(offsets, 2, 3), amplitudes, jnp.asarray(tables))

    return jax.shard_map(
        local,
        mesh=mesh,
        in_specs=(
            P(None, "row", "col"),
            P(),
            P("row", "col", None, None),
            P("row", "col", None, None, None),
        ),
        out_specs=P(None, "row", "col"),
        check_vma=False,
    )
```

```python
import functools
import math

import jax
import jax.numpy as jnp
import ml_dtypes
import numpy as np
from jax import lax
from jax.experimental import pallas as pl
from jax.experimental.pallas import tpu as pltpu
from jax.sharding import PartitionSpec as P

WIN = 256
HALF = 128
HALO = 128
ITERS = 2
SMOOTH = 0.25
RIDGE = 0.1
MESH = pl.DeviceIdType.MESH

NEIGHBOURS = [(a, b) for a in (-1, 0, 1) for b in (-1, 0, 1) if (a, b) != (0, 0)]


def dft_tables():
    n = np.arange(HALF)[None, :]
    m = np.arange(HALF)[:, None]
    blocks = []
    for freq in (2 * m, 2 * m + 1):
        angle = -2.0 * math.pi * ((freq * n) % WIN) / WIN
        re, im = np.cos(angle) / 16.0, np.sin(angle) / 16.0
        blocks.append(np.block([[re, -im], [im, re]]))
    out = []
    for block in (blocks[0], blocks[1], blocks[0].T, blocks[1].T):
        high = block.astype(ml_dtypes.bfloat16)
        low = (block - high.astype(np.float64)).astype(ml_dtypes.bfloat16)
        out += [high, low]
    order = np.concatenate([np.arange(0, WIN, 2), np.arange(1, WIN, 2)])
    perm = (order[:, None] == np.arange(WIN)[None, :]).astype(ml_dtypes.bfloat16)
    out += [perm, perm.T]
    return np.stack(out)


def split(x):
    high = x.astype(jnp.bfloat16)
    low = (x - high.astype(jnp.float32)).astype(jnp.bfloat16)
    return high, low


def dot(a, b):
    return jnp.dot(a, b, preferred_element_type=jnp.float32)


def left(tab, index, x):
    high, low = split(x)
    th, tl = tab[2 * index], tab[2 * index + 1]
    return dot(jnp.concatenate([th, th, tl], axis=1), jnp.concatenate([high, low, high], axis=0))


def right(x, tab, index):
    high, low = split(x)
    th, tl = tab[2 * index], tab[2 * index + 1]
    return dot(jnp.concatenate([high, low, high], axis=1), jnp.concatenate([th, th, tl], axis=0))


def digits(size, part):
    return (size // part, part) if size > part else (1, size)


Z_LEN = 8
CHUNKS = 2


class Message:
    def __init__(self, pool, device, send_if, recv_if, src, dst):
        send, recv, index = pool[0], pool[1], pool[2]
        pool[2] += 1
        self.send_if, self.recv_if = send_if, recv_if
        self.copy = pltpu.make_async_remote_copy(
            src, dst, send.at[index], recv.at[index], device_id=device, device_id_type=MESH
        )

    def _when(self, cond, action):
        if cond is None:
            action()
        else:
            pl.when(cond)(action)

    def start(self):
        self._when(self.send_if, self.copy.start)

    def recv(self):
        self._when(self.recv_if, self.copy.wait_recv)

    def sent(self):
        self._when(self.send_if, self.copy.wait_send)


def kernel(
    n_row, n_col, n_pos,
    spec, probe_in, off, amp_in, tab_in,
    out,
    span_a, span_b, grad, wide, pad, light, inv, probe, amp, tab, noff,
    corner_in, core_in, row_in, col_in, relay_strip, relay_row, peak_out, peak_in,
    local_sem, off_sem, send_sem, recv_sem, peak_send, peak_recv,
):
    r, c = lax.axis_index("row"), lax.axis_index("col")
    f32 = jnp.float32
    spans = (span_a, span_b)
    lane = lax.broadcasted_iota(jnp.int32, (1, HALF), 1)
    pool = [send_sem, recv_sem, 0]

    odd = r % 2
    near = pl.multiple_of(HALO + HALF - HALF * odd, HALF)
    far = pl.multiple_of(HALO + HALF * odd, HALF)
    inner = pl.multiple_of((HALO + WIN) * (1 - odd), HALF)
    outer = pl.multiple_of((HALO + WIN) * odd, HALF)
    inner_there, outer_there = outer, inner
    partner = {"row": r + 1 - 2 * odd, "col": c}
    r_out = r - 1 + 2 * odd
    has_outer = (r_out >= 0) & (r_out < n_row)
    beyond = {"row": r_out, "col": c}

    def exists(dr, dc):
        ok = None
        for index, step, size in ((r, dr, n_row), (c, dc, n_col)):
            if step:
                here = (index + step >= 0) & (index + step < size)
                ok = here if ok is None else ok & here
        return ok

    def col_ok(x):
        return (x >= 0) & (x < n_col)

    ra, rb = digits(n_row, 4)
    ca, cb = digits(n_col, Z_LEN)
    groups = []
    for size, place in (
        (rb, lambda j: {"row": (r // rb) * rb + (r % rb + j) % rb, "col": c}),
        (cb, lambda j: {"row": r, "col": (c // cb) * cb + (c % cb + j) % cb}),
        (ra, lambda j: {"row": ((r // rb + j) % ra) * rb + r % rb, "col": c}),
        (ca, lambda j: {"row": r, "col": ((c // cb + j) % ca) * cb + c % cb}),
    ):
        groups.append([(j, place(j)) for j in range(1, size)])

    for k in range(9):
        for p in range(n_pos):
            for d in range(2):
                if k == 4:
                    noff[k, d, p] = off[0, 0, d, p]
                else:
                    noff[k, d, p] = 4096

    for k in range(2):
        for cond, place in (
            (jnp.logical_not(has_outer), (slice(None), pl.ds(outer, HALO))),
            (c == 0, (0, pl.ds(0, 512))),
            (c == n_col - 1, (3, pl.ds(0, 512))),
        ):
            @pl.when(cond)
            def _(k=k, place=place):
                ref = spans[k].at[(slice(None),) + place + (slice(None),)]
                ref[...] = jnp.zeros(ref.shape, f32)

    barrier = pltpu.get_barrier_semaphore()
    total = 0
    for dr, dc in NEIGHBOURS:
        here = exists(dr, dc)
        total = total + here.astype(jnp.int32)

        @pl.when(here)
        def _(dr=dr, dc=dc):
            pl.semaphore_signal(barrier, inc=1, device_id={"row": r + dr, "col": c + dc}, device_id_type=MESH)

    for group in groups:
        for j, place in group:
            pl.semaphore_signal(barrier, inc=1, device_id=place, device_id_type=MESH)
            total = total + 1

    copies = [
        pltpu.make_async_copy(spec.at[:, :, pl.ds(0, HALF)], span_a.at[:, 1, pl.ds(HALO, WIN), :], local_sem.at[0]),
        pltpu.make_async_copy(spec.at[:, :, pl.ds(HALF, HALF)], span_a.at[:, 2, pl.ds(HALO, WIN), :], local_sem.at[1]),
        pltpu.make_async_copy(probe_in, probe, local_sem.at[2]),
        pltpu.make_async_copy(tab_in, tab, local_sem.at[3]),
        pltpu.make_async_copy(amp_in.at[0, 0], amp, local_sem.at[4]),
    ]
    for copy in copies:
        copy.start()
    copies[0].wait()
    copies[1].wait()

    pl.semaphore_wait(barrier, total)

    def along(dc, src, dst, cond=None):
        send_if, recv_if = col_ok(c + dc), col_ok(c - dc)
        if cond is not None:
            send_if, recv_if = send_if & cond(c), recv_if & cond(c - dc)
        return Message(pool, {"row": r, "col": c + dc}, send_if, recv_if, src, dst)

    def strip(dc, src, dst, start, count, relay, also=None):
        edge = Z_LEN - 1 if dc > 0 else 0
        one, two = dc - dc * Z_LEN, dc * Z_LEN
        both = lambda f: f if also is None else (lambda x: f(x) & also)
        inside = both(lambda x: x % Z_LEN != edge)
        cross = both(lambda x: (x % Z_LEN == edge) & col_ok(x + dc))
        rows = pl.ds(start, count)
        whole = along(dc, src.at[:, rows, :], dst.at[:, rows, :], inside)
        pairs = []
        size = count // CHUNKS
        for n in range(CHUNKS):
            rows = pl.ds(start + n * size, size)
            slot = relay.at[:, pl.ds(n * size, size), :]
            pairs.append(
                (
                    along(one, src.at[:, rows, :], slot, cross),
                    along(two, slot, dst.at[:, rows, :], lambda x: cross(x - one)),
                )
            )
        return whole, pairs

    def planes(x):
        return ((x % Z_LEN == Z_LEN - 1) & (x < n_col - 1)) | ((x % Z_LEN == 0) & (x > 0))

    def outer_rows(src, dst, relay):
        half, size = HALF // 2, HALF // 2 // CHUNKS
        end_here = planes(c)
        first_end = c % Z_LEN == 0
        passes = ((c % Z_LEN == Z_LEN - 2) & planes(c + 1)) | ((c % Z_LEN == 1) & planes(c - 1))
        to_relay = {"row": r, "col": c + jnp.where(first_end, 1, -1)}
        from_relay = {"row": r_out, "col": c + jnp.where(c % Z_LEN == 1, -1, 1)}

        def part(start, count, cond):
            rows = pl.ds(start, count)
            return Message(pool, beyond, cond, cond, src.at[:, :, rows, :], dst.at[:, :, rows, :])

        direct = [part(0, half, has_outer), part(half, half, has_outer & jnp.logical_not(end_here))]
        pairs = []
        for n in range(CHUNKS):
            rows = pl.ds(half + n * size, size)
            slot = relay.at[:, :, pl.ds(n * size, size), :]
            pairs.append(
                (
                    Message(pool, to_relay, has_outer & end_here, has_outer & passes, src.at[:, :, rows, :], slot),
                    Message(pool, from_relay, has_outer & passes, has_outer & end_here, slot, dst.at[:, :, rows, :]),
                )
            )
        return direct, pairs

    both_tiles = pl.ds(1, 2)

    def widen(k):
        span = spans[k]
        relays, direct, far_strips, corners, cores = [], [], [], [], []
        for i, (dc, here, there) in enumerate(((1, 2, 0), (-1, 1, 3))):
            whole, pairs = strip(dc, span.at[:, here], span.at[:, there], far, HALF, relay_strip.at[k, i])
            far_strips.append(whole)
            relays += pairs
            direct.append(
                along(dc, span.at[:, here, pl.ds(near, HALF), :], span.at[:, there, pl.ds(near, HALF), :])
            )
            rows = pl.ds(outer, HALF)
            corners.append(
                along(dc, span.at[:, here, rows, :], span.at[:, there, rows, :], lambda x: has_outer)
            )
        mirrored = pl.ds(inner_there, HALF)
        for t in (0, 3):
            cores.append(
                Message(
                    pool, partner, None, None, span.at[:, t, pl.ds(near, HALF), :], span.at[:, t, mirrored, :]
                )
            )
        row_core = Message(
            pool, partner, None, None,
            span.at[:, both_tiles, pl.ds(near, HALF), :], span.at[:, both_tiles, mirrored, :],
        )
        row_far, row_relays = outer_rows(
            span.at[:, both_tiles, pl.ds(far, HALF), :],
            span.at[:, both_tiles, pl.ds(outer_there, HALF), :],
            relay_row.at[k],
        )

        def start_far():
            for first, _ in relays + row_relays:
                first.start()
            for m in row_far + far_strips:
                m.start()

        def start_near():
            row_core.start()
            for m in direct:
                m.start()

        def relay(n):
            for pairs in (relays, row_relays):
                for first, second in pairs[n::CHUNKS]:
                    first.recv()
                    second.start()

        def middle():
            for m in row_far:
                m.recv()
            for _, second in row_relays:
                second.recv()
            row_core.recv()
            for m in corners:
                m.start()
            for m in direct:
                m.recv()
            for m in cores:
                m.start()

        def end():
            for m in far_strips + cores + corners:
                m.recv()
            for _, second in relays:
                second.recv()
            for m in [row_core] + row_far + direct + far_strips + cores + corners:
                m.sent()
            for first, second in relays + row_relays:
                first.sent()
                second.sent()

        return start_near, start_far, relay, middle, end

    start_near, start_far, relay, middle, end = widen(0)
    off_copies = []
    for i, (dr, dc) in enumerate(NEIGHBOURS):
        slot = (-dr + 1) * 3 + (-dc + 1)
        copy = pltpu.make_async_remote_copy(
            off.at[0, 0], noff.at[slot], off_sem.at[0, i], off_sem.at[1, i],
            device_id={"row": r + dr, "col": c + dc}, device_id_type=MESH,
        )
        pl.when(exists(dr, dc))(copy.start)
        off_copies.append((copy, dr, dc))
    start_far()
    start_near()

    def clear(ref, count):
        def body(i, _):
            ref[i] = jnp.zeros(ref.shape[1:], f32)
            return 0

        lax.fori_loop(0, count, body, 0)

    clear(pad, 7)
    copies[2].wait()
    for t in range(2):
        cols = pl.ds(t * HALF, HALF)
        pad[2 + t, pl.ds(WIN, WIN), :] = probe[0, :, cols] * probe[0, :, cols] + probe[1, :, cols] * probe[1, :, cols]

    def clear_wide(i, _):
        p, rest = i // 12, i % 12
        wide[p, rest // 6, rest % 6] = jnp.zeros((3 * WIN, HALF), f32)
        return 0

    lax.fori_loop(0, n_pos * 12, clear_wide, 0)
    for n in range(CHUNKS):
        relay(n)
    for copy, dr, dc in off_copies:
        pl.when(exists(dr, dc))(copy.wait_send)
        pl.when(exists(-dr, -dc))(copy.wait_recv)

    light[...] = jnp.zeros(light.shape, f32)

    for dr, dc in [(0, 0)] + NEIGHBOURS:
        place = (dr + 1) * 3 + dc + 1
        first, count = {-1: (0, HALF), 0: (0, WIN), 1: (HALF, HALF)}[dr]
        tiles_in = {-1: (0,), 0: (0, 1), 1: (1,)}[dc]

        def add_light(p, _, place=place, dr=dr, dc=dc, first=first, count=count, tiles_in=tiles_in):
            top = jnp.clip(noff[place, 0, p] + dr * WIN, -WIN, WIN)
            side = jnp.clip(noff[place, 1, p] + dc * WIN, -WIN, WIN)
            rows = pl.ds(WIN - top + first, count)
            start_col = WIN - side
            q, s = start_col // HALF, start_col % HALF
            turn = (HALF - s) % HALF
            keep = lane < HALF - s
            rolled = {
                j: pltpu.roll(pad[q + j, rows, :], turn, 1) for j in range(tiles_in[0], tiles_in[-1] + 2)
            }
            here = pl.ds(first, count)
            for t in tiles_in:
                light[t, here, :] = light[t, here, :] + jnp.where(keep, rolled[t], rolled[t + 1])
            return 0

        lax.fori_loop(0, n_pos, add_light, 0)

    peak = jnp.max(light[...].reshape(2 * WIN // 8, 8, HALF), axis=0)

    def peak_start(phase, value):
        peak_out[phase] = value
        items = []
        for j, place in groups[phase]:
            copy = pltpu.make_async_remote_copy(
                peak_out.at[phase], peak_in.at[phase, j], peak_send.at[phase, j], peak_recv.at[phase, j],
                device_id=place, device_id_type=MESH,
            )
            copy.start()
            items.append(copy)
        return items

    def peak_finish(phase, items):
        for copy in items:
            copy.wait()
        value = peak_out[phase]
        for j, _ in groups[phase]:
            value = jnp.maximum(value, peak_in[phase, j])
        return value

    items = peak_start(0, peak)
    middle()

    copies[3].wait()
    copies[4].wait()

    def order_amp(p, _):
        rows = tab[8]
        high, low = split(amp[p])
        x = dot(jnp.concatenate([rows, rows], axis=1), jnp.concatenate([high, low], axis=0))
        high, low = split(x)
        cols = tab[9]
        amp[p] = dot(jnp.concatenate([high, low], axis=1), jnp.concatenate([cols, cols], axis=0))
        return 0

    lax.fori_loop(0, n_pos, order_amp, 0)
    peak = peak_finish(0, items)
    items = peak_start(1, peak)
    end()

    def cat(a, b, axis):
        return jnp.concatenate([a, b], axis=axis)

    def windows(k):
        every = range(n_pos)
        pr, pi = probe[0], probe[1]
        shift = [side % HALF for side in sides]
        sums, difs = [], []
        for p in every:
            rows = pl.ds(tops[p], WIN)
            turn = (HALF - shift[p]) % HALF
            keep = lane < HALF - shift[p]
            patch = []
            for part in range(2):
                rolled = [
                    pltpu.roll(spans[k][part, jnp.minimum(tiles[p] + j, 3), rows, :], turn, 1) for j in range(3)
                ]
                patch.append(cat(jnp.where(keep, rolled[0], rolled[1]), jnp.where(keep, rolled[1], rolled[2]), 1))
            er = pr * patch[0] - pi * patch[1]
            ei = pr * patch[1] + pi * patch[0]
            sums.append(cat(er[:HALF] + er[HALF:], ei[:HALF] + ei[HALF:], 0))
            difs.append(cat(er[:HALF] - er[HALF:], ei[:HALF] - ei[HALF:], 0))
        even = [left(tab, 0, x) for x in sums]
        odd_ = [left(tab, 1, x) for x in difs]
        sums, difs = [], []
        for p in every:
            xr = cat(even[p][:HALF], odd_[p][:HALF], 0)
            xi = cat(even[p][HALF:], odd_[p][HALF:], 0)
            sums.append(cat(xr[:, :HALF] + xr[:, HALF:], xi[:, :HALF] + xi[:, HALF:], 1))
            difs.append(cat(xr[:, :HALF] - xr[:, HALF:], xi[:, :HALF] - xi[:, HALF:], 1))
        back = []
        for index, xs in ((0, sums), (1, difs)):
            far_field = [right(x, tab, 2 + index) for x in xs]
            scaled = []
            for p in every:
                fr, fi = far_field[p][:, :HALF], far_field[p][:, HALF:]
                factor = 1.0 - amp[p, :, pl.ds(index * HALF, HALF)] * lax.rsqrt(fr * fr + fi * fi + SMOOTH)
                scaled.append(cat(factor * fr, factor * fi, 1))
            back.append([right(x, tab, index) for x in scaled])
        even, odd_ = [], []
        for p in every:
            lo, hi = back[0][p] + back[1][p], back[0][p] - back[1][p]
            xr = cat(lo[:, :HALF], hi[:, :HALF], 1)
            xi = cat(lo[:, HALF:], hi[:, HALF:], 1)
            even.append(left(tab, 2, cat(xr[:HALF], xi[:HALF], 0)))
            odd_.append(left(tab, 3, cat(xr[HALF:], xi[HALF:], 0)))
        zero = jnp.zeros((WIN, HALF), f32)
        for p in every:
            lo, hi = even[p] + odd_[p], even[p] - odd_[p]
            br = cat(lo[:HALF], hi[:HALF], 0)
            bi = cat(lo[HALF:], hi[HALF:], 0)
            g = (pr * br + pi * bi, pr * bi - pi * br)
            past = lane >= shift[p]
            for part in range(2):
                one = pltpu.roll(g[part][:, :HALF], shift[p], 1)
                two = pltpu.roll(g[part][:, HALF:], shift[p], 1)
                wide[p, part, 2, pl.ds(WIN, WIN), :] = jnp.where(past, one, zero)
                wide[p, part, 3, pl.ds(WIN, WIN), :] = jnp.where(past, two, one)
                wide[p, part, 4, pl.ds(WIN, WIN), :] = jnp.where(past, zero, two)

    tops = [off[0, 0, 0, p] + HALO for p in range(n_pos)]
    sides = [off[0, 0, 1, p] + HALO for p in range(n_pos)]
    tiles = [side // HALF for side in sides]

    def gather(k, t, start):
        for part in range(2):
            acc = None
            for p in range(n_pos):
                piece = wide[p, part, 2 + t - tiles[p], pl.ds(WIN - tops[p] + start, HALF), :]
                acc = piece if acc is None else acc + piece
            grad[k, part, t, pl.ds(start, HALF), :] = acc

    def accumulate(k, t, start, ref):
        for part in range(2):
            rows = pl.ds(start, HALF)
            grad[k, part, t, rows, :] = grad[k, part, t, rows, :] + ref[part]

    def fold(k, before, on_near, on_far):
        g = grad.at[k]
        relays, direct, far_strips, corners, cores = [], [], [], [], []
        for i, (dc, here) in enumerate(((1, 3), (-1, 0))):
            whole, pairs = strip(dc, g.at[:, here], col_in.at[k, i], far, HALF, relay_strip.at[ITERS + k, i])
            far_strips.append(whole)
            relays += pairs
            direct.append(
                along(dc, g.at[:, here, pl.ds(near, HALF), :], col_in.at[k, i, :, pl.ds(near, HALF), :])
            )
            corners.append(
                along(dc, g.at[:, here, pl.ds(outer, HALF), :], corner_in.at[k, i], lambda x: has_outer)
            )
            cores.append(
                Message(pool, partner, None, None, g.at[:, here, pl.ds(inner, HALF), :], core_in.at[k, i])
            )
        row_far, row_relays = outer_rows(
            g.at[:, both_tiles, pl.ds(outer, HALF), :], row_in.at[k, 0], relay_row.at[ITERS + k]
        )
        row_core = Message(pool, partner, None, None, g.at[:, both_tiles, pl.ds(inner, HALF), :], row_in.at[k, 1])

        for t in (0, 3):
            gather(k, t, outer)
        for m in corners:
            m.start()
        for t in (0, 3):
            gather(k, t, inner)
        for m in cores:
            m.start()
        for t in (0, 3):
            gather(k, t, far)
        for first, _ in relays:
            first.start()
        for m in far_strips:
            m.start()
        for t in (0, 3):
            gather(k, t, near)
        for t in (1, 2):
            gather(k, t, outer)
        for i, m in enumerate(cores):
            m.recv()
            accumulate(k, (3, 0)[i], near, core_in.at[k, i])
        for m in direct:
            m.start()
        for t in (1, 2):
            gather(k, t, inner)
        row_core.start()
        for i, m in enumerate(corners):
            m.recv()

            @pl.when(has_outer & col_ok(c - (1, -1)[i]))
            def _(i=i):
                accumulate(k, 1 + i, outer, corner_in.at[k, i])
        for first, _ in row_relays:
            first.start()
        for m in row_far:
            m.start()
        for first, second in relays:
            first.recv()
            second.start()
        for t in (1, 2):
            gather(k, t, near)
            gather(k, t, far)
        for first, second in row_relays:
            first.recv()
            second.start()
        before()
        row_core.recv()
        for t in (1, 2):
            accumulate(k, t, near, row_in.at[k, 1, :, t - 1])

        def columns(start):
            for i in range(2):
                @pl.when(col_ok(c - (1, -1)[i]))
                def _(i=i):
                    accumulate(k, 1 + i, start, col_in.at[k, i, :, pl.ds(start, HALF), :])

        for m in direct:
            m.recv()
        columns(near)
        on_near()
        for m in far_strips:
            m.recv()
        for _, second in relays:
            second.recv()
        columns(far)
        for m in row_far:
            m.recv()
        for _, second in row_relays:
            second.recv()

        @pl.when(has_outer)
        def _():
            for t in (1, 2):
                accumulate(k, t, far, row_in.at[k, 0, :, t - 1])

        on_far()

        def end():
            for m in [row_core] + row_far + direct + far_strips + corners + cores:
                m.sent()
            for first, second in relays + row_relays:
                first.sent()
                second.sent()

        return end

    def update(k, start):
        rows = pl.ds(start, HALF)
        for t in range(2):
            for part in range(2):
                step = grad[k, part, 1 + t, rows, :] * inv[t, pl.ds(start - HALO, HALF), :]
                new = spans[k][part, 1 + t, rows, :] - step
                if k + 1 < ITERS:
                    spans[k + 1][part, 1 + t, rows, :] = new
                else:
                    out[part, pl.ds(start - HALO, HALF), pl.ds(t * HALF, HALF)] = new

    for k in range(ITERS):
        last = k + 1 == ITERS
        if k == 0:
            peak = peak_finish(1, items)
            items = peak_start(2, peak)
        windows(k)
        if k == 0:
            peak = peak_finish(2, items)
            items = peak_start(3, peak)

        def before():
            if k == 0:
                inv[...] = 1.0 / (light[...] + RIDGE * jnp.max(peak_finish(3, items)))

        if not last:
            start_near, start_far, relay, middle, end = widen(k + 1)

        def on_near():
            update(k, near)
            if not last:
                start_near()

        def on_far():
            update(k, far)
            if not last:
                start_far()

        end_fold = fold(k, before, on_near, on_far)
        if not last:
            for n in range(CHUNKS):
                relay(n)
            middle()
            end()
        end_fold()


def solution(mesh):
    n_row, n_col = mesh.shape["row"], mesh.shape["col"]
    tables = dft_tables()

    def local(specimen, probe_field, offsets, amplitudes):
        n_pos = offsets.shape[2]
        vmem = lambda *shape: pltpu.VMEM(shape, jnp.float32)
        dma = lambda *shape: pltpu.SemaphoreType.DMA(shape)
        return pl.pallas_call(
            functools.partial(kernel, n_row, n_col, n_pos),
            out_shape=jax.ShapeDtypeStruct((2, WIN, WIN), jnp.float32),
            in_specs=[
                pl.BlockSpec(memory_space=pl.ANY),
                pl.BlockSpec(memory_space=pl.ANY),
                pl.BlockSpec(memory_space=pltpu.SMEM),
                pl.BlockSpec(memory_space=pl.ANY),
                pl.BlockSpec(memory_space=pl.ANY),
            ],
            out_specs=pl.BlockSpec(memory_space=pltpu.VMEM),
            scratch_shapes=[
                vmem(2, 4, 512, HALF),
                vmem(2, 4, 512, HALF),
                vmem(ITERS, 2, 4, 512, HALF),
                vmem(n_pos, 2, 6, 3 * WIN, HALF),
                vmem(7, 3 * WIN, HALF),
                vmem(2, WIN, HALF),
                vmem(2, WIN, HALF),
                vmem(2, WIN, WIN),
                vmem(n_pos, WIN, WIN),
                pltpu.VMEM((10, WIN, WIN), jnp.bfloat16),
                pltpu.SMEM((9, 2, n_pos), jnp.int32),
                vmem(ITERS, 2, 2, HALF, HALF),
                vmem(ITERS, 2, 2, HALF, HALF),
                vmem(ITERS, 2, 2, 2, HALO, HALF),
                vmem(ITERS, 2, 2, 512, HALF),
                vmem(2 * ITERS, 2, 2, HALF, HALF),
                vmem(2 * ITERS, 2, 2, HALF // 2, HALF),
                vmem(4, 8, HALF),
                vmem(4, 8, 8, HALF),
                dma(5),
                dma(2, 8),
                dma(112),
                dma(112),
                dma(4, 8),
                dma(4, 8),
            ],
            compiler_params=pltpu.CompilerParams(
                collective_id=0, has_side_effects=True, vmem_limit_bytes=56 * 1024 * 1024
            ),
        )(specimen, probe_field, jnp.swapaxes(offsets, 2, 3), amplitudes, jnp.asarray(tables))

    return jax.shard_map(
        local,
        mesh=mesh,
        in_specs=(
            P(None, "row", "col"),
            P(),
            P("row", "col", None, None),
            P("row", "col", None, None, None),
        ),
        out_specs=P(None, "row", "col"),
        check_vma=False,
    )
```

```python
import functools
import math

import jax
import jax.numpy as jnp
import ml_dtypes
import numpy as np
from jax import lax
from jax.experimental import pallas as pl
from jax.experimental.pallas import tpu as pltpu
from jax.sharding import PartitionSpec as P

WIN = 256
HALF = 128
HALO = 128
ITERS = 2
SMOOTH = 0.25
RIDGE = 0.1
MESH = pl.DeviceIdType.MESH

NEIGHBOURS = [(a, b) for a in (-1, 0, 1) for b in (-1, 0, 1) if (a, b) != (0, 0)]


def dft_tables():
    n = np.arange(HALF)[None, :]
    m = np.arange(HALF)[:, None]
    blocks = []
    for freq in (2 * m, 2 * m + 1):
        angle = -2.0 * math.pi * ((freq * n) % WIN) / WIN
        re, im = np.cos(angle) / 16.0, np.sin(angle) / 16.0
        blocks.append(np.block([[re, -im], [im, re]]))
    out = []
    for block in (blocks[0], blocks[1], blocks[0].T, blocks[1].T):
        high = block.astype(ml_dtypes.bfloat16)
        low = (block - high.astype(np.float64)).astype(ml_dtypes.bfloat16)
        out += [high, low]
    order = np.concatenate([np.arange(0, WIN, 2), np.arange(1, WIN, 2)])
    perm = (order[:, None] == np.arange(WIN)[None, :]).astype(ml_dtypes.bfloat16)
    out += [perm, perm.T]
    return np.stack(out)


def split(x):
    high = x.astype(jnp.bfloat16)
    low = (x - high.astype(jnp.float32)).astype(jnp.bfloat16)
    return high, low


def dot(a, b):
    return jnp.dot(a, b, preferred_element_type=jnp.float32)


def left(tab, index, x):
    high, low = split(x)
    th, tl = tab[2 * index], tab[2 * index + 1]
    return dot(jnp.concatenate([th, th, tl], axis=1), jnp.concatenate([high, low, high], axis=0))


def right(x, tab, index):
    high, low = split(x)
    th, tl = tab[2 * index], tab[2 * index + 1]
    return dot(jnp.concatenate([high, low, high], axis=1), jnp.concatenate([th, th, tl], axis=0))


def digits(size, part):
    return (size // part, part) if size > part else (1, size)


Z_LEN = 8
CHUNKS = 2


class Message:
    def __init__(self, pool, device, send_if, recv_if, src, dst):
        send, recv, index = pool[0], pool[1], pool[2]
        pool[2] += 1
        self.send_if, self.recv_if = send_if, recv_if
        self.copy = pltpu.make_async_remote_copy(
            src, dst, send.at[index], recv.at[index], device_id=device, device_id_type=MESH
        )

    def _when(self, cond, action):
        if cond is None:
            action()
        else:
            pl.when(cond)(action)

    def start(self):
        self._when(self.send_if, self.copy.start)

    def recv(self):
        self._when(self.recv_if, self.copy.wait_recv)

    def sent(self):
        self._when(self.send_if, self.copy.wait_send)


def kernel(
    n_row, n_col, n_pos,
    spec, probe_in, off, amp_in, tab_in,
    out,
    span_a, span_b, grad, wide, pad, light, inv, probe, amp, tab, noff,
    corner_in, core_in, row_in, col_in, relay_strip, relay_row, peak_out, peak_in,
    local_sem, off_sem, send_sem, recv_sem, peak_send, peak_recv,
):
    r, c = lax.axis_index("row"), lax.axis_index("col")
    f32 = jnp.float32
    spans = (span_a, span_b)
    lane = lax.broadcasted_iota(jnp.int32, (1, HALF), 1)
    pool = [send_sem, recv_sem, 0]

    odd = r % 2
    near = pl.multiple_of(HALO + HALF - HALF * odd, HALF)
    far = pl.multiple_of(HALO + HALF * odd, HALF)
    inner = pl.multiple_of((HALO + WIN) * (1 - odd), HALF)
    outer = pl.multiple_of((HALO + WIN) * odd, HALF)
    inner_there, outer_there = outer, inner
    partner = {"row": r + 1 - 2 * odd, "col": c}
    r_out = r - 1 + 2 * odd
    has_outer = (r_out >= 0) & (r_out < n_row)
    beyond = {"row": r_out, "col": c}

    def exists(dr, dc):
        ok = None
        for index, step, size in ((r, dr, n_row), (c, dc, n_col)):
            if step:
                here = (index + step >= 0) & (index + step < size)
                ok = here if ok is None else ok & here
        return ok

    def col_ok(x):
        return (x >= 0) & (x < n_col)

    ra, rb = digits(n_row, 4)
    ca, cb = digits(n_col, Z_LEN)
    groups = []
    for size, place in (
        (rb, lambda j: {"row": (r // rb) * rb + (r % rb + j) % rb, "col": c}),
        (cb, lambda j: {"row": r, "col": (c // cb) * cb + (c % cb + j) % cb}),
        (ra, lambda j: {"row": ((r // rb + j) % ra) * rb + r % rb, "col": c}),
        (ca, lambda j: {"row": r, "col": ((c // cb + j) % ca) * cb + c % cb}),
    ):
        groups.append([(j, place(j)) for j in range(1, size)])

    for k in range(9):
        for p in range(n_pos):
            for d in range(2):
                if k == 4:
                    noff[k, d, p] = off[0, 0, d, p]
                else:
                    noff[k, d, p] = 4096

    for k in range(2):
        for cond, place in (
            (jnp.logical_not(has_outer), (slice(None), pl.ds(outer, HALO))),
            (c == 0, (0, pl.ds(0, 512))),
            (c == n_col - 1, (3, pl.ds(0, 512))),
        ):
            @pl.when(cond)
            def _(k=k, place=place):
                ref = spans[k].at[(slice(None),) + place + (slice(None),)]
                ref[...] = jnp.zeros(ref.shape, f32)

    barrier = pltpu.get_barrier_semaphore()
    total = 0
    for dr, dc in NEIGHBOURS:
        here = exists(dr, dc)
        total = total + here.astype(jnp.int32)

        @pl.when(here)
        def _(dr=dr, dc=dc):
            pl.semaphore_signal(barrier, inc=1, device_id={"row": r + dr, "col": c + dc}, device_id_type=MESH)

    for group in groups:
        for j, place in group:
            pl.semaphore_signal(barrier, inc=1, device_id=place, device_id_type=MESH)
            total = total + 1

    copies = [
        pltpu.make_async_copy(spec.at[:, :, pl.ds(0, HALF)], span_a.at[:, 1, pl.ds(HALO, WIN), :], local_sem.at[0]),
        pltpu.make_async_copy(spec.at[:, :, pl.ds(HALF, HALF)], span_a.at[:, 2, pl.ds(HALO, WIN), :], local_sem.at[1]),
        pltpu.make_async_copy(probe_in, probe, local_sem.at[2]),
        pltpu.make_async_copy(tab_in, tab, local_sem.at[3]),
        pltpu.make_async_copy(amp_in.at[0, 0], amp, local_sem.at[4]),
    ]
    for copy in copies:
        copy.start()
    copies[0].wait()
    copies[1].wait()

    pl.semaphore_wait(barrier, total)

    def along(dc, src, dst, cond=None):
        send_if, recv_if = col_ok(c + dc), col_ok(c - dc)
        if cond is not None:
            send_if, recv_if = send_if & cond(c), recv_if & cond(c - dc)
        return Message(pool, {"row": r, "col": c + dc}, send_if, recv_if, src, dst)

    def strip(dc, src, dst, start, count, relay, also=None):
        edge = Z_LEN - 1 if dc > 0 else 0
        one, two = dc - dc * Z_LEN, dc * Z_LEN
        both = lambda f: f if also is None else (lambda x: f(x) & also)
        inside = both(lambda x: x % Z_LEN != edge)
        cross = both(lambda x: (x % Z_LEN == edge) & col_ok(x + dc))
        rows = pl.ds(start, count)
        whole = along(dc, src.at[:, rows, :], dst.at[:, rows, :], inside)
        pairs = []
        size = count // CHUNKS
        for n in range(CHUNKS):
            rows = pl.ds(start + n * size, size)
            slot = relay.at[:, pl.ds(n * size, size), :]
            pairs.append(
                (
                    along(one, src.at[:, rows, :], slot, cross),
                    along(two, slot, dst.at[:, rows, :], lambda x: cross(x - one)),
                )
            )
        return whole, pairs

    def planes(x):
        return ((x % Z_LEN == Z_LEN - 1) & (x < n_col - 1)) | ((x % Z_LEN == 0) & (x > 0))

    def outer_rows(src, dst, relay):
        half, size = HALF // 2, HALF // 2 // CHUNKS
        end_here = planes(c)
        first_end = c % Z_LEN == 0
        passes = ((c % Z_LEN == Z_LEN - 2) & planes(c + 1)) | ((c % Z_LEN == 1) & planes(c - 1))
        to_relay = {"row": r, "col": c + jnp.where(first_end, 1, -1)}
        from_relay = {"row": r_out, "col": c + jnp.where(c % Z_LEN == 1, -1, 1)}

        def part(start, count, cond):
            rows = pl.ds(start, count)
            return Message(pool, beyond, cond, cond, src.at[:, :, rows, :], dst.at[:, :, rows, :])

        direct = [part(0, half, has_outer), part(half, half, has_outer & jnp.logical_not(end_here))]
        pairs = []
        for n in range(CHUNKS):
            rows = pl.ds(half + n * size, size)
            slot = relay.at[:, :, pl.ds(n * size, size), :]
            pairs.append(
                (
                    Message(pool, to_relay, has_outer & end_here, has_outer & passes, src.at[:, :, rows, :], slot),
                    Message(pool, from_relay, has_outer & passes, has_outer & end_here, slot, dst.at[:, :, rows, :]),
                )
            )
        return direct, pairs

    both_tiles = pl.ds(1, 2)

    def widen(k):
        span = spans[k]
        relays, direct, far_strips, corners, cores = [], [], [], [], []
        for i, (dc, here, there) in enumerate(((1, 2, 0), (-1, 1, 3))):
            whole, pairs = strip(dc, span.at[:, here], span.at[:, there], far, HALF, relay_strip.at[k, i])
            far_strips.append(whole)
            relays += pairs
            direct.append(
                along(dc, span.at[:, here, pl.ds(near, HALF), :], span.at[:, there, pl.ds(near, HALF), :])
            )
            rows = pl.ds(outer, HALF)
            corners.append(
                along(dc, span.at[:, here, rows, :], span.at[:, there, rows, :], lambda x: has_outer)
            )
        mirrored = pl.ds(inner_there, HALF)
        for t in (0, 3):
            cores.append(
                Message(
                    pool, partner, None, None, span.at[:, t, pl.ds(near, HALF), :], span.at[:, t, mirrored, :]
                )
            )
        row_core = Message(
            pool, partner, None, None,
            span.at[:, both_tiles, pl.ds(near, HALF), :], span.at[:, both_tiles, mirrored, :],
        )
        row_far, row_relays = outer_rows(
            span.at[:, both_tiles, pl.ds(far, HALF), :],
            span.at[:, both_tiles, pl.ds(outer_there, HALF), :],
            relay_row.at[k],
        )

        def start_far():
            for first, _ in relays + row_relays:
                first.start()
            for m in row_far + far_strips:
                m.start()

        def start_near():
            row_core.start()
            for m in direct:
                m.start()

        def relay(n):
            for pairs in (relays, row_relays):
                for first, second in pairs[n::CHUNKS]:
                    first.recv()
                    second.start()

        def middle():
            for m in row_far:
                m.recv()
            for _, second in row_relays:
                second.recv()
            row_core.recv()
            for m in corners:
                m.start()
            for m in direct:
                m.recv()
            for m in cores:
                m.start()

        def end():
            for m in far_strips + cores + corners:
                m.recv()
            for _, second in relays:
                second.recv()
            for m in [row_core] + row_far + direct + far_strips + cores + corners:
                m.sent()
            for first, second in relays + row_relays:
                first.sent()
                second.sent()

        return start_near, start_far, relay, middle, end

    start_near, start_far, relay, middle, end = widen(0)
    off_copies = []
    for i, (dr, dc) in enumerate(NEIGHBOURS):
        slot = (-dr + 1) * 3 + (-dc + 1)
        copy = pltpu.make_async_remote_copy(
            off.at[0, 0], noff.at[slot], off_sem.at[0, i], off_sem.at[1, i],
            device_id={"row": r + dr, "col": c + dc}, device_id_type=MESH,
        )
        pl.when(exists(dr, dc))(copy.start)
        off_copies.append((copy, dr, dc))
    start_far()
    start_near()

    def clear(ref, count):
        def body(i, _):
            ref[i] = jnp.zeros(ref.shape[1:], f32)
            return 0

        lax.fori_loop(0, count, body, 0)

    clear(pad, 7)
    copies[2].wait()
    for t in range(2):
        cols = pl.ds(t * HALF, HALF)
        pad[2 + t, pl.ds(WIN, WIN), :] = probe[0, :, cols] * probe[0, :, cols] + probe[1, :, cols] * probe[1, :, cols]

    def clear_wide(i, _):
        p, rest = i // 12, i % 12
        wide[p, rest // 6, rest % 6] = jnp.zeros((3 * WIN, HALF), f32)
        return 0

    for n in range(CHUNKS):
        relay(n)
    for copy, dr, dc in off_copies:
        pl.when(exists(dr, dc))(copy.wait_send)
        pl.when(exists(-dr, -dc))(copy.wait_recv)

    light[...] = jnp.zeros(light.shape, f32)

    for dr, dc in [(0, 0)] + NEIGHBOURS:
        place = (dr + 1) * 3 + dc + 1
        first, count = {-1: (0, HALF), 0: (0, WIN), 1: (HALF, HALF)}[dr]
        tiles_in = {-1: (0,), 0: (0, 1), 1: (1,)}[dc]

        def add_light(p, _, place=place, dr=dr, dc=dc, first=first, count=count, tiles_in=tiles_in):
            top = jnp.clip(noff[place, 0, p] + dr * WIN, -WIN, WIN)
            side = jnp.clip(noff[place, 1, p] + dc * WIN, -WIN, WIN)
            rows = pl.ds(WIN - top + first, count)
            start_col = WIN - side
            q, s = start_col // HALF, start_col % HALF
            turn = (HALF - s) % HALF
            keep = lane < HALF - s
            rolled = {
                j: pltpu.roll(pad[q + j, rows, :], turn, 1) for j in range(tiles_in[0], tiles_in[-1] + 2)
            }
            here = pl.ds(first, count)
            for t in tiles_in:
                light[t, here, :] = light[t, here, :] + jnp.where(keep, rolled[t], rolled[t + 1])
            return 0

        lax.fori_loop(0, n_pos, add_light, 0)

    peak = jnp.max(light[...].reshape(2 * WIN // 8, 8, HALF), axis=0)

    def peak_start(phase, value):
        peak_out[phase] = value
        items = []
        for j, place in groups[phase]:
            copy = pltpu.make_async_remote_copy(
                peak_out.at[phase], peak_in.at[phase, j], peak_send.at[phase, j], peak_recv.at[phase, j],
                device_id=place, device_id_type=MESH,
            )
            copy.start()
            items.append(copy)
        return items

    def peak_finish(phase, items):
        for copy in items:
            copy.wait()
        value = peak_out[phase]
        for j, _ in groups[phase]:
            value = jnp.maximum(value, peak_in[phase, j])
        return value

    items = peak_start(0, peak)
    middle()

    lax.fori_loop(0, n_pos * 12, clear_wide, 0)

    copies[3].wait()
    copies[4].wait()

    def order_amp(p, _):
        rows = tab[8]
        high, low = split(amp[p])
        x = dot(jnp.concatenate([rows, rows], axis=1), jnp.concatenate([high, low], axis=0))
        high, low = split(x)
        cols = tab[9]
        amp[p] = dot(jnp.concatenate([high, low], axis=1), jnp.concatenate([cols, cols], axis=0))
        return 0

    lax.fori_loop(0, n_pos, order_amp, 0)
    peak = peak_finish(0, items)
    items = peak_start(1, peak)
    end()

    def cat(a, b, axis):
        return jnp.concatenate([a, b], axis=axis)

    def windows(k):
        every = range(n_pos)
        pr, pi = probe[0], probe[1]
        shift = [side % HALF for side in sides]
        sums, difs = [], []
        for p in every:
            rows = pl.ds(tops[p], WIN)
            turn = (HALF - shift[p]) % HALF
            keep = lane < HALF - shift[p]
            patch = []
            for part in range(2):
                rolled = [
                    pltpu.roll(spans[k][part, jnp.minimum(tiles[p] + j, 3), rows, :], turn, 1) for j in range(3)
                ]
                patch.append(cat(jnp.where(keep, rolled[0], rolled[1]), jnp.where(keep, rolled[1], rolled[2]), 1))
            er = pr * patch[0] - pi * patch[1]
            ei = pr * patch[1] + pi * patch[0]
            sums.append(cat(er[:HALF] + er[HALF:], ei[:HALF] + ei[HALF:], 0))
            difs.append(cat(er[:HALF] - er[HALF:], ei[:HALF] - ei[HALF:], 0))
        even = [left(tab, 0, x) for x in sums]
        odd_ = [left(tab, 1, x) for x in difs]
        sums, difs = [], []
        for p in every:
            xr = cat(even[p][:HALF], odd_[p][:HALF], 0)
            xi = cat(even[p][HALF:], odd_[p][HALF:], 0)
            sums.append(cat(xr[:, :HALF] + xr[:, HALF:], xi[:, :HALF] + xi[:, HALF:], 1))
            difs.append(cat(xr[:, :HALF] - xr[:, HALF:], xi[:, :HALF] - xi[:, HALF:], 1))
        back = []
        for index, xs in ((0, sums), (1, difs)):
            far_field = [right(x, tab, 2 + index) for x in xs]
            scaled = []
            for p in every:
                fr, fi = far_field[p][:, :HALF], far_field[p][:, HALF:]
                factor = 1.0 - amp[p, :, pl.ds(index * HALF, HALF)] * lax.rsqrt(fr * fr + fi * fi + SMOOTH)
                scaled.append(cat(factor * fr, factor * fi, 1))
            back.append([right(x, tab, index) for x in scaled])
        even, odd_ = [], []
        for p in every:
            lo, hi = back[0][p] + back[1][p], back[0][p] - back[1][p]
            xr = cat(lo[:, :HALF], hi[:, :HALF], 1)
            xi = cat(lo[:, HALF:], hi[:, HALF:], 1)
            even.append(left(tab, 2, cat(xr[:HALF], xi[:HALF], 0)))
            odd_.append(left(tab, 3, cat(xr[HALF:], xi[HALF:], 0)))
        zero = jnp.zeros((WIN, HALF), f32)
        for p in every:
            lo, hi = even[p] + odd_[p], even[p] - odd_[p]
            br = cat(lo[:HALF], hi[:HALF], 0)
            bi = cat(lo[HALF:], hi[HALF:], 0)
            g = (pr * br + pi * bi, pr * bi - pi * br)
            past = lane >= shift[p]
            for part in range(2):
                one = pltpu.roll(g[part][:, :HALF], shift[p], 1)
                two = pltpu.roll(g[part][:, HALF:], shift[p], 1)
                wide[p, part, 2, pl.ds(WIN, WIN), :] = jnp.where(past, one, zero)
                wide[p, part, 3, pl.ds(WIN, WIN), :] = jnp.where(past, two, one)
                wide[p, part, 4, pl.ds(WIN, WIN), :] = jnp.where(past, zero, two)

    tops = [off[0, 0, 0, p] + HALO for p in range(n_pos)]
    sides = [off[0, 0, 1, p] + HALO for p in range(n_pos)]
    tiles = [side // HALF for side in sides]

    def gather(k, t, start):
        for part in range(2):
            acc = None
            for p in range(n_pos):
                piece = wide[p, part, 2 + t - tiles[p], pl.ds(WIN - tops[p] + start, HALF), :]
                acc = piece if acc is None else acc + piece
            grad[k, part, t, pl.ds(start, HALF), :] = acc

    def accumulate(k, t, start, ref):
        for part in range(2):
            rows = pl.ds(start, HALF)
            grad[k, part, t, rows, :] = grad[k, part, t, rows, :] + ref[part]

    def fold(k, before, on_near, on_far):
        g = grad.at[k]
        relays, direct, far_strips, corners, cores = [], [], [], [], []
        for i, (dc, here) in enumerate(((1, 3), (-1, 0))):
            whole, pairs = strip(dc, g.at[:, here], col_in.at[k, i], far, HALF, relay_strip.at[ITERS + k, i])
            far_strips.append(whole)
            relays += pairs
            direct.append(
                along(dc, g.at[:, here, pl.ds(near, HALF), :], col_in.at[k, i, :, pl.ds(near, HALF), :])
            )
            corners.append(
                along(dc, g.at[:, here, pl.ds(outer, HALF), :], corner_in.at[k, i], lambda x: has_outer)
            )
            cores.append(
                Message(pool, partner, None, None, g.at[:, here, pl.ds(inner, HALF), :], core_in.at[k, i])
            )
        row_far, row_relays = outer_rows(
            g.at[:, both_tiles, pl.ds(outer, HALF), :], row_in.at[k, 0], relay_row.at[ITERS + k]
        )
        row_core = Message(pool, partner, None, None, g.at[:, both_tiles, pl.ds(inner, HALF), :], row_in.at[k, 1])

        for t in (0, 3):
            gather(k, t, outer)
        for m in corners:
            m.start()
        for t in (0, 3):
            gather(k, t, inner)
        for m in cores:
            m.start()
        for t in (0, 3):
            gather(k, t, far)
        for first, _ in relays:
            first.start()
        for m in far_strips:
            m.start()
        for t in (0, 3):
            gather(k, t, near)
        for t in (1, 2):
            gather(k, t, outer)
        for i, m in enumerate(cores):
            m.recv()
            accumulate(k, (3, 0)[i], near, core_in.at[k, i])
        for m in direct:
            m.start()
        for t in (1, 2):
            gather(k, t, inner)
        row_core.start()
        for first, second in relays:
            first.recv()
            second.start()
        for i, m in enumerate(corners):
            m.recv()

            @pl.when(has_outer & col_ok(c - (1, -1)[i]))
            def _(i=i):
                accumulate(k, 1 + i, outer, corner_in.at[k, i])
        for first, _ in row_relays:
            first.start()
        for m in row_far:
            m.start()
        for t in (1, 2):
            gather(k, t, near)
            gather(k, t, far)
        for first, second in row_relays:
            first.recv()
            second.start()
        before()
        row_core.recv()
        for t in (1, 2):
            accumulate(k, t, near, row_in.at[k, 1, :, t - 1])

        def columns(start):
            for i in range(2):
                @pl.when(col_ok(c - (1, -1)[i]))
                def _(i=i):
                    accumulate(k, 1 + i, start, col_in.at[k, i, :, pl.ds(start, HALF), :])

        for m in direct:
            m.recv()
        columns(near)
        on_near()
        for m in far_strips:
            m.recv()
        for _, second in relays:
            second.recv()
        columns(far)
        for m in row_far:
            m.recv()
        for _, second in row_relays:
            second.recv()

        @pl.when(has_outer)
        def _():
            for t in (1, 2):
                accumulate(k, t, far, row_in.at[k, 0, :, t - 1])

        on_far()

        def end():
            for m in [row_core] + row_far + direct + far_strips + corners + cores:
                m.sent()
            for first, second in relays + row_relays:
                first.sent()
                second.sent()

        return end

    def update(k, start):
        rows = pl.ds(start, HALF)
        for t in range(2):
            for part in range(2):
                step = grad[k, part, 1 + t, rows, :] * inv[t, pl.ds(start - HALO, HALF), :]
                new = spans[k][part, 1 + t, rows, :] - step
                if k + 1 < ITERS:
                    spans[k + 1][part, 1 + t, rows, :] = new
                else:
                    out[part, pl.ds(start - HALO, HALF), pl.ds(t * HALF, HALF)] = new

    for k in range(ITERS):
        last = k + 1 == ITERS
        if k == 0:
            peak = peak_finish(1, items)
            items = peak_start(2, peak)
        windows(k)
        if k == 0:
            peak = peak_finish(2, items)
            items = peak_start(3, peak)

        def before():
            if k == 0:
                inv[...] = 1.0 / (light[...] + RIDGE * jnp.max(peak_finish(3, items)))

        if not last:
            start_near, start_far, relay, middle, end = widen(k + 1)

        def on_near():
            update(k, near)
            if not last:
                start_near()

        def on_far():
            update(k, far)
            if not last:
                start_far()

        end_fold = fold(k, before, on_near, on_far)
        if not last:
            for n in range(CHUNKS):
                relay(n)
            middle()
            end()
        end_fold()


def solution(mesh):
    n_row, n_col = mesh.shape["row"], mesh.shape["col"]
    tables = dft_tables()

    def local(specimen, probe_field, offsets, amplitudes):
        n_pos = offsets.shape[2]
        vmem = lambda *shape: pltpu.VMEM(shape, jnp.float32)
        dma = lambda *shape: pltpu.SemaphoreType.DMA(shape)
        return pl.pallas_call(
            functools.partial(kernel, n_row, n_col, n_pos),
            out_shape=jax.ShapeDtypeStruct((2, WIN, WIN), jnp.float32),
            in_specs=[
                pl.BlockSpec(memory_space=pl.ANY),
                pl.BlockSpec(memory_space=pl.ANY),
                pl.BlockSpec(memory_space=pltpu.SMEM),
                pl.BlockSpec(memory_space=pl.ANY),
                pl.BlockSpec(memory_space=pl.ANY),
            ],
            out_specs=pl.BlockSpec(memory_space=pltpu.VMEM),
            scratch_shapes=[
                vmem(2, 4, 512, HALF),
                vmem(2, 4, 512, HALF),
                vmem(ITERS, 2, 4, 512, HALF),
                vmem(n_pos, 2, 6, 3 * WIN, HALF),
                vmem(7, 3 * WIN, HALF),
                vmem(2, WIN, HALF),
                vmem(2, WIN, HALF),
                vmem(2, WIN, WIN),
                vmem(n_pos, WIN, WIN),
                pltpu.VMEM((10, WIN, WIN), jnp.bfloat16),
                pltpu.SMEM((9, 2, n_pos), jnp.int32),
                vmem(ITERS, 2, 2, HALF, HALF),
                vmem(ITERS, 2, 2, HALF, HALF),
                vmem(ITERS, 2, 2, 2, HALO, HALF),
                vmem(ITERS, 2, 2, 512, HALF),
                vmem(2 * ITERS, 2, 2, HALF, HALF),
                vmem(2 * ITERS, 2, 2, HALF // 2, HALF),
                vmem(4, 8, HALF),
                vmem(4, 8, 8, HALF),
                dma(5),
                dma(2, 8),
                dma(112),
                dma(112),
                dma(4, 8),
                dma(4, 8),
            ],
            compiler_params=pltpu.CompilerParams(
                collective_id=0, has_side_effects=True, vmem_limit_bytes=56 * 1024 * 1024
            ),
        )(specimen, probe_field, jnp.swapaxes(offsets, 2, 3), amplitudes, jnp.asarray(tables))

    return jax.shard_map(
        local,
        mesh=mesh,
        in_specs=(
            P(None, "row", "col"),
            P(),
            P("row", "col", None, None),
            P("row", "col", None, None, None),
        ),
        out_specs=P(None, "row", "col"),
        check_vma=False,
    )
```
